256 devices in a mesh: grp: 8 (over y, x_lo), pen: 32 (over x_hi, z, core).
Axes of the slice: x: 4 (x_hi: 2, x_lo: 2; x = x_hi * 2 + x_lo), y: 4, z: 8, core: 2. Of those that a mesh axis runs over, the one named last changes fastest.
Arguments:
- field: float32 [8, 64, 64, 64, 128], P('grp', 'pen'), may hold values from -6 to 6
- upstream: bfloat16 [8, 64, 64, 64, 128], P('grp', 'pen'), may hold values from -6 to 6
- mode_weights: bfloat16 [16, 32, 16, 2, 128, 128], P(None, 'pen', 'grp'), may hold values from -1.5 to 1.5
- skip_weight: float32 [128, 128], replicated, may hold values from -0.5 to 0.5
- channel_bias: float32 [128], replicated, may hold values from -3 to 3
Outputs:
- output: bfloat16 [8, 64, 64, 64, 128], P('grp', 'pen')
- weight_grad: bfloat16 [16, 32, 16, 2, 128, 128], P(None, 'pen', 'grp')
The draws below stay inside these ranges and needn't reach their ends.
All inputs are finite; a program needn't handle non-finite values.
Results may differ from the reference program's by a relative error of at most 0.006.
Values may be sent and summed in bfloat16 or wider, within the bound.
A program may use at most 64 MiB of HBM per device.

```python
import jax
import jax.numpy as jnp
from jax import lax

C = 128
NX = 64
NY = 64
NZ = 64
MX = 16
MY = 32
MZ = 16
SAMPLES = 8


def shard_levels(own_key, extent, shards, low, largest):
    loudness = 1.0
    for axis_at, parts in shards:
        draws = jax.random.uniform(jax.random.fold_in(jax.random.fold_in(own_key, 6), axis_at), (parts,), jnp.float32, low / len(shards), largest / len(shards))
        loudness = loudness * jnp.repeat(jnp.exp(draws), extent[axis_at] // parts).reshape((-1,) + (1,) * (len(extent) - 1 - axis_at))
    return loudness


def gaussian(rng, shape, deviation, limit, split=(), held_as=jnp.bfloat16):
    loudness = shard_levels(rng, shape, split, -0.22, 0.18) if split else 1.0
    array = jax.random.normal(rng, shape, jnp.float32) * deviation * loudness
    return jnp.minimum(jnp.maximum(array, -limit), limit).astype(held_as)


def setup_inputs(seed: int = 0) -> dict:
    arg_keys = jax.random.split(jax.random.key(seed), 6)
    return {
        "field": gaussian(arg_keys[0], (SAMPLES, NX, NY, NZ, C), 1.0, 6.0, ((0, 8), (1, 32)), jnp.float32),
        "upstream": gaussian(arg_keys[1], (SAMPLES, NX, NY, NZ, C), 1.0, 6.0, ((0, 8), (1, 32))),
        "mode_weights": gaussian(arg_keys[2], (MX, MY, MZ, 2, C, C), (4 * MX * MY * MZ * C // (NX * NY * NZ)) ** -0.5, 1.5, ((1, 32), (2, 8))),
        "skip_weight": gaussian(arg_keys[3], (C, C), C ** -0.5, 0.5, (), jnp.float32),
        "channel_bias": gaussian(arg_keys[4], (C,), 0.5, 3.0, (), jnp.float32),
    }


def kept_indices(length, number):
    lower_half = jnp.arange(number // 2, dtype=jnp.int32)
    upper_half = jnp.arange(length - (number - number // 2), length, dtype=jnp.int32)
    return jnp.concatenate([lower_half, upper_half]).astype(jnp.int32)

def take_modes(values):
    spec = jnp.fft.rfftn(values, axes=(0, 1, 2), norm='ortho')
    kept_first = kept_indices(NX, MX)
    kept_second = kept_indices(NY, MY)
    spec = spec[kept_first][:, kept_second][:, :, :MZ]
    return jnp.stack([jnp.real(spec), jnp.imag(spec)], axis=3).astype(jnp.float32)

def make_field(modes):
    kept_first = kept_indices(NX, MX)
    kept_second = kept_indices(NY, MY)
    kept_third = jnp.arange(MZ, dtype=jnp.int32)
    blank = jnp.zeros((NX, NY, NZ // 2 + 1, C), jnp.float32)
    where_first = kept_first[:, None, None]
    where_second = kept_second[None, :, None]
    where_third = kept_third[None, None, :]
    real_full = blank.at[where_first, where_second, where_third].set(modes[:, :, :, 0])
    imag_full = blank.at[where_first, where_second, where_third].set(modes[:, :, :, 1])
    spec = lax.complex(real_full, imag_full)
    return jnp.fft.irfftn(spec, s=(NX, NY, NZ), axes=(0, 1, 2), norm='ortho').astype(jnp.float32)

def paired(spectrum):
    real_part = spectrum[..., 0:1, :]
    imag_part = spectrum[..., 1:2, :]
    real_row = jnp.concatenate([real_part, -imag_part], axis=-2)
    imag_row = jnp.concatenate([imag_part, real_part], axis=-2)
    return jnp.stack([real_row, imag_row], axis=-3)

def exact_gelu(values):
    return jax.nn.gelu(values, approximate=False)

def reference(field, upstream, mode_weights, skip_weight, channel_bias):
    depth_weight = jnp.where(jnp.arange(MZ) == 0, 1.0, 2.0).astype(jnp.float32)
    spectrum = lax.map(take_modes, field).astype(jnp.bfloat16)
    paired_spec = paired(spectrum)
    paired_first = jnp.moveaxis(paired_spec, 1, 0)

    def mix_one(pieces):
        spec_piece, weight_piece = pieces
        return jnp.einsum('byzpqi,yzqio->byzpo', spec_piece.astype(jnp.float32), weight_piece.astype(jnp.float32))
    mixed_modes = jnp.moveaxis(lax.map(mix_one, (paired_first, mode_weights)), 0, 1)

    def sample_pass(pieces):
        sample_field, sample_modes, sample_up = pieces
        spectral = make_field(sample_modes)
        skip_part = jnp.dot(sample_field, skip_weight, precision=lax.Precision.HIGHEST)
        pre_act = spectral + skip_part + channel_bias
        output = exact_gelu(pre_act).astype(jnp.bfloat16)
        _, pullback = jax.vjp(exact_gelu, pre_act)
        pre_grad = pullback(sample_up.astype(jnp.float32))[0]
        mode_grad = take_modes(pre_grad) * depth_weight[None, None, :, None, None]
        return (output, mode_grad.astype(jnp.bfloat16))
    output, mode_grad = lax.map(sample_pass, (field, mixed_modes, upstream))
    grad_first = jnp.moveaxis(mode_grad, 1, 0)

    def grad_one(pieces):
        spec_piece, grad_piece = pieces
        summed = jnp.einsum('byzpqi,byzpo->yzqio', spec_piece.astype(jnp.float32), grad_piece.astype(jnp.float32))
        return summed.astype(jnp.bfloat16)
    weight_grad = lax.map(grad_one, (paired_first, grad_first))
    return (output, weight_grad)
```

```python
import functools
import math

import jax
import jax.numpy as jnp
import ml_dtypes
import numpy as np
from jax import lax
from jax.experimental import pallas as pl
from jax.experimental.pallas import tpu as pltpu
from jax.sharding import PartitionSpec as P

MESH = pl.DeviceIdType.MESH
f32 = jnp.float32
bf16 = jnp.bfloat16


def rotation(angle, inverse):
    cosine, sine = np.cos(angle), np.sin(angle)
    sign = -1.0 if inverse else 1.0
    real_row = np.stack([cosine, sign * sine], axis=-1)
    imag_row = np.stack([-sign * sine, cosine], axis=-1)
    return np.stack([real_row, imag_row], axis=-2) / 8.0


def halves(table, axis):
    high = table.astype(ml_dtypes.bfloat16)
    low = (table - high.astype(np.float64)).astype(ml_dtypes.bfloat16)
    return np.concatenate([high, low], axis=axis)


def make_tables():
    turn = 2.0 * math.pi / 64.0
    cell = np.arange(64)
    depth = turn * (np.arange(16)[:, None] * cell[None, :] % 64)
    weight = np.where(np.arange(16) == 0, 1.0, 2.0)[:, None, None]
    depth = np.stack([np.cos(depth), -np.sin(depth)], axis=1) / 8.0
    by_parity = lambda t: t.reshape(8, 2, 2, 64).transpose(1, 0, 2, 3)
    eye = np.eye
    t1 = np.einsum("carz,yw->cayrwz", by_parity(depth), eye(4)).reshape(128, 256)
    t6 = np.einsum("carz,yw->yzcawr", by_parity(depth * weight), eye(4)).reshape(256, 128)
    ky = np.arange(16)[None, :] - 16 * np.arange(2)[:, None]
    row = turn * (ky[:, :, None] * cell % 64)
    t2 = np.einsum("hdyrs,ab->dahrbys", rotation(row, False), eye(2)).reshape(128, 256)
    t5 = np.einsum("hdyrs,ab->ayrdbhs", rotation(row, True), eye(4)).reshape(512, 256)
    kx = np.where(np.arange(16) < 8, np.arange(16), np.arange(16) - 16)
    plane = turn * (kx[:, None] * cell % 64)
    forward = rotation(plane, False).reshape(16, 2, 16, 2, 2, 2)
    backward = rotation(plane, True).reshape(16, 2, 16, 2, 2, 2)
    t3 = np.einsum("kXserv,ab,hi->Xeahkrsbiv", forward, eye(4), eye(2)).reshape(2, 2, 256, 256)
    t4 = np.einsum("kXserv,ab,hi->Xesahribkv", backward, eye(4), eye(2)).reshape(2, 2, 256, 256)
    swap = np.eye(256).reshape(8, 32, 256).transpose(1, 0, 2).reshape(256, 256)
    return (
        halves(t1, 0),
        halves(t2, 0),
        halves(t3, 2),
        halves(t4, 2),
        halves(t5, 0),
        halves(t6, 1),
        np.concatenate([swap, swap], axis=1).astype(ml_dtypes.bfloat16),
        np.ascontiguousarray(swap.T).astype(ml_dtypes.bfloat16),
    )


def dot(left, right):
    return jnp.dot(left, right, preferred_element_type=f32)


def split(values):
    high = values.astype(bf16)
    return high, (values - high.astype(f32)).astype(bf16)


def dot_split(table, values):
    rows = table.shape[0] // 2
    both = dot(table, jnp.concatenate(split(values), axis=1))
    return both[:rows, :128] + both[:rows, 128:] + both[rows:, :128]


def dot_exact(table, values):
    rows = table.shape[0] // 2
    both = dot(table, values)
    return both[:rows] + both[rows:]


SCALED = (
    0.11283793162135076,
    0.11283476245314182,
    0.10392192770562217,
    0.0842669599289443,
    0.07073040277585074,
    -0.002833797179664962,
    0.08457735964663142,
    -0.09147177273287684,
    0.025136288482206462,
)


def gelu_pair(v):
    bell = jnp.exp(-0.5 * (v * v))
    t = 1.0 / (1.0 + 0.282842712474619 * jnp.abs(v))
    series = jnp.full_like(t, SCALED[-1] * 1.0)
    for coefficient in SCALED[-2::-1]:
        series = series * t + coefficient
    tail = bell * (t * series)
    phi = jnp.where(v >= 0, 1.0 - tail, tail)
    return v * phi, phi + v * (bell * (1.0 / math.sqrt(2.0 * math.pi)))


def kernel(
    field_hbm, up_hbm, weight_hbm, skip_hbm, bias_hbm, t1_hbm, t2_hbm, t3_hbm, t4_hbm, t5_hbm, t6_hbm, gather_hbm, scatter_hbm,
    out_hbm, grad_hbm,
    field, up, weight, skip, bias, t1, t2, t3, t4, t5, t6, gather, scatter,
    base, out, grad, zbuf, ybuf, rows, pairs, mixed,
    ring_send, ring_recv, wide_send, wide_recv, back_send, back_recv,
    load_sem, ring_ssem, ring_rsem, wide_ssem, wide_rsem, back_ssem, back_rsem, store_sem,
):
    g = lax.axis_index("grp")
    p = lax.axis_index("pen")
    x_hi = p // 16
    d = lax.rem(p, 16)
    w = g * 2 + x_hi

    def ring_peer(i):
        to = lax.rem(d + i, 16)
        return to, (g, x_hi * 16 + to)

    def wide_peer(i):
        to = lax.rem(w + i, 16)
        return to, (to // 2, lax.rem(to, 2) * 16 + d)

    barrier = pltpu.get_barrier_semaphore()

    def greet(i, carry):
        for peer in (ring_peer, wide_peer):
            pl.semaphore_signal(barrier, inc=1, device_id=peer(i)[1], device_id_type=MESH)
        return carry

    lax.fori_loop(1, 16, greet, 0)

    loads = []

    def load(source, target):
        copy = pltpu.make_async_copy(source, target, load_sem.at[len(loads)])
        copy.start()
        loads.append(copy)
        return copy

    t1_load = load(t1_hbm, t1)
    quarters = [
        load(field_hbm.at[:, pl.ds(n * 1024, 1024), :], field.at[:, pl.ds(n * 1024, 1024), :]) for n in range(4)
    ]
    t2_load = load(t2_hbm, t2)
    skip_load = load(skip_hbm, skip)
    bias_load = load(bias_hbm, bias)
    t3_load = load(t3_hbm.at[x_hi], t3)
    gather_load = load(gather_hbm, gather)
    weight_load = load(weight_hbm, weight)
    scatter_load = load(scatter_hbm, scatter)
    t4_load = load(t4_hbm.at[x_hi], t4)
    t5_load = load(t5_hbm, t5)
    t6_load = load(t6_hbm, t6)
    up_load = load(up_hbm, up)

    def ring_start(n, e, c):
        source, target = ring_send.at[n, e, c], ring_recv.at[n, e, c]
        pltpu.make_async_copy(source.at[d], target.at[d], ring_rsem.at[n, e, c]).start()

        def send(i, carry):
            to, device = ring_peer(i)
            pltpu.make_async_remote_copy(
                src_ref=source.at[to],
                dst_ref=target.at[d],
                send_sem=ring_ssem.at[n, e, c],
                recv_sem=ring_rsem.at[n, e, c],
                device_id=device,
                device_id_type=MESH,
            ).start()
            return carry

        lax.fori_loop(1, 16, send, 0)

    def wide_start(n, c):
        source, target = wide_send.at[n, c], wide_recv.at[n, c]
        slot = x_hi * 8 + g
        pltpu.make_async_copy(source.at[w], target.at[slot], wide_rsem.at[n, c]).start()

        def send(i, carry):
            to, device = wide_peer(i)
            pltpu.make_async_remote_copy(
                src_ref=source.at[to],
                dst_ref=target.at[slot],
                send_sem=wide_ssem.at[n, c],
                recv_sem=wide_rsem.at[n, c],
                device_id=device,
                device_id_type=MESH,
            ).start()
            return carry

        lax.fori_loop(1, 16, send, 0)

    def back_start(c):
        source, target = back_send.at[c], back_recv.at[c]
        slot = (g // 4) * 8 + x_hi * 4 + lax.rem(g, 4)
        pltpu.make_async_copy(source.at[g], target.at[slot], back_rsem.at[c]).start()

        def send(i, carry):
            to, device = wide_peer(i)
            pltpu.make_async_remote_copy(
                src_ref=source.at[to // 2],
                dst_ref=target.at[slot],
                send_sem=back_ssem.at[c],
                recv_sem=back_rsem.at[c],
                device_id=device,
                device_id_type=MESH,
            ).start()
            return carry

        lax.fori_loop(1, 16, send, 0)

    def drain(buffer, semaphore):
        pltpu.make_async_copy(buffer, buffer, semaphore).wait()

    def depth_step(e, m, values):
        tile = dot_split(t1[...], values).reshape(16, 8, 128)
        zbuf[e, :, pl.ds(pl.multiple_of(m * 8, 8), 8), :] = tile

    def row_step(n, e, c):
        for q in range(2):
            tiles = []
            for half in range(2):
                first = c * 8 + q * 4 + half * 2
                values = zbuf[e, first : first + 2].reshape(256, 128)
                tiles.append(dot_split(t2[...], values).reshape(16, 8, 128))
            ring_send[n, e, c, :, q] = jnp.concatenate(tiles, axis=1).astype(bf16)

    def plane_step(n, c):
        for q in range(2):
            total = dot_exact(t3[0], ring_recv[n, 0, c, :, q].reshape(256, 128))
            total += dot_exact(t3[1], ring_recv[n, 1, c, :, q].reshape(256, 128))
            wide_send[n // 2, c, q * 8 : q * 8 + 8] = total.reshape(8, 32, 128)

    def collect(n, c):
        summed = (wide_recv[n, c, 0:8] + wide_recv[n, c, 8:16]).reshape(256, 128)
        rows[...] = dot(gather[...], jnp.concatenate(split(summed), axis=0))

    t1_load.wait()
    for n in range(4):
        quarters[n].wait()

        def depth_loop(m, carry):
            for e in range(2):
                values = field[e, pl.ds(pl.multiple_of(m * 256, 256), 256), :]
                depth_step(e, m, values)
            return carry

        lax.fori_loop(n * 4, n * 4 + 4, depth_loop, 0)
    t2_load.wait()
    for c in range(2):
        for e in range(2):
            row_step(0, e, c)
            if c == 0 and e == 0:
                pl.semaphore_wait(barrier, 30)
            ring_start(0, e, c)

    skip_load.wait()
    bias_load.wait()
    skip_row = jnp.concatenate(split(skip[...]), axis=1)
    skip_both = jnp.concatenate([skip_row, skip_row], axis=0)

    def skip_loop(m, carry):
        for e in range(2):
            here = pl.ds(pl.multiple_of(m * 256, 256), 256)
            both = dot(jnp.concatenate(split(field[e, here, :]), axis=1), skip_both)
            base[e, here, :] = both[:, :128] + both[:, 128:] + bias[...]
        return carry

    lax.fori_loop(0, 16, skip_loop, 0)

    t3_load.wait()
    for c in range(2):
        for e in range(2):
            drain(ring_recv.at[0, e, c], ring_rsem.at[0, e, c])
        plane_step(0, c)
        wide_start(0, c)

    gather_load.wait()
    weight_load.wait()
    scatter_load.wait()
    for c in range(2):
        drain(wide_recv.at[0, c], wide_rsem.at[0, c])
        collect(0, c)

        def mix_loop(m, carry):
            for i in range(4):
                k = m * 4 + i
                real = rows[pl.ds(pl.multiple_of(k * 16, 16), 8), :]
                imag = rows[pl.ds(pl.multiple_of(k * 16 + 8, 8), 8), :]
                upper = jnp.concatenate([real, -imag], axis=1)
                lower = jnp.concatenate([imag, real], axis=1)
                paired = jnp.concatenate([upper, lower], axis=0).astype(bf16)
                pairs[c, k] = paired
                mixed[pl.ds(pl.multiple_of(k * 16, 16), 16), :] = dot(paired, weight[k, c]).astype(bf16)
            return carry

        lax.fori_loop(0, 4, mix_loop, 0)
        back_send[c] = dot(scatter[...], mixed[...]).astype(bf16).reshape(8, 32, 128)
        back_start(c)

    t4_load.wait()
    for c in range(2):
        drain(back_recv.at[c], back_rsem.at[c])
        for q in range(2):
            values = back_recv[c, q * 8 : q * 8 + 8].reshape(256, 128)
            for e in range(2):
                ring_send[1, e, c, :, q] = dot_exact(t4[e], values).reshape(16, 16, 128).astype(bf16)
        ring_start(1, 0, c)
    ring_start(1, 1, 0)
    ring_start(1, 1, 1)

    t5_load.wait()
    t6_load.wait()
    up_load.wait()
    stores = []
    for e in range(2):
        for c in range(2):
            drain(ring_recv.at[1, e, c], ring_rsem.at[1, e, c])
            for q in range(2):
                first = c * 8 + q * 4
                values = ring_recv[1, e, c, :, q].reshape(256, 128)
                ybuf[first : first + 4] = dot_exact(t5[...], values).reshape(4, 128, 128)

        def cell_loop(m, carry):
            values = ybuf[:, pl.ds(pl.multiple_of(m * 8, 8), 8), :].reshape(128, 128)
            half = jnp.concatenate(split(values), axis=1)
            both = dot(t6[...], jnp.concatenate([half, half], axis=0))
            here = pl.ds(pl.multiple_of(m * 256, 256), 256)
            value, slope = gelu_pair(both[:, :128] + both[:, 128:] + base[e, here, :])
            out[e, here, :] = value.astype(bf16)
            depth_step(e, m, slope * up[e, here, :].astype(f32))
            return carry

        lax.fori_loop(0, 16, cell_loop, 0)
        store = pltpu.make_async_copy(out.at[e], out_hbm.at[e], store_sem.at[e])
        store.start()
        stores.append(store)
        for c in range(2):
            row_step(2, e, c)
            ring_start(2, e, c)

    for c in range(2):
        for e in range(2):
            drain(ring_recv.at[2, e, c], ring_rsem.at[2, e, c])
        plane_step(2, c)
        wide_start(1, c)

    for c in range(2):
        drain(wide_recv.at[1, c], wide_rsem.at[1, c])
        collect(1, c)
        scale = jnp.where(g == 0, 1.0, 2.0).astype(f32) if c == 0 else f32(2.0)

        def grad_loop(m, carry):
            for i in range(4):
                k = m * 4 + i
                cotangent = (rows[pl.ds(pl.multiple_of(k * 16, 16), 16), :] * scale).astype(bf16)
                product = lax.dot_general(
                    pairs[c, k], cotangent, (((0,), (0,)), ((), ())), preferred_element_type=f32
                )
                grad[c, k] = product.astype(bf16)
            return carry

        lax.fori_loop(0, 4, grad_loop, 0)
        store = pltpu.make_async_copy(grad.at[c], grad_hbm.at[:, c], store_sem.at[2 + c])
        store.start()
        stores.append(store)

    for n in range(3):
        for e in range(2):
            for c in range(2):
                drain(ring_send.at[n, e, c, pl.ds(0, 15)], ring_ssem.at[n, e, c])
    for n in range(2):
        for c in range(2):
            drain(wide_send.at[n, c, pl.ds(0, 15)], wide_ssem.at[n, c])
    for c in range(2):
        drain(back_recv.at[c, pl.ds(0, 15)], back_ssem.at[c])
    for store in stores:
        store.wait()


def shards(tables, field, upstream, mode_weights, skip_weight, channel_bias):
    anywhere = pl.BlockSpec(memory_space=pl.ANY)
    out, grad = pl.pallas_call(
        kernel,
        out_shape=(
            jax.ShapeDtypeStruct((2, 4096, 128), bf16),
            jax.ShapeDtypeStruct((16, 2, 256, 128), bf16),
        ),
        in_specs=[anywhere] * 13,
        out_specs=(anywhere, anywhere),
        scratch_shapes=[
            pltpu.VMEM((2, 4096, 128), f32),
            pltpu.VMEM((2, 4096, 128), bf16),
            pltpu.VMEM((16, 2, 256, 128), bf16),
            pltpu.VMEM((128, 128), f32),
            pltpu.VMEM((1, 128), f32),
            pltpu.VMEM((256, 256), bf16),
            pltpu.VMEM((256, 256), bf16),
            pltpu.VMEM((2, 512, 256), bf16),
            pltpu.VMEM((2, 512, 256), bf16),
            pltpu.VMEM((1024, 256), bf16),
            pltpu.VMEM((256, 256), bf16),
            pltpu.VMEM((256, 512), bf16),
            pltpu.VMEM((256, 256), bf16),
            pltpu.VMEM((2, 4096, 128), f32),
            pltpu.VMEM((2, 4096, 128), bf16),
            pltpu.VMEM((2, 16, 256, 128), bf16),
            pltpu.VMEM((2, 16, 128, 128), f32),
            pltpu.VMEM((16, 128, 128), f32),
            pltpu.VMEM((256, 128), f32),
            pltpu.VMEM((2, 16, 16, 256), bf16),
            pltpu.VMEM((256, 128), bf16),
            pltpu.VMEM((3, 2, 2, 16, 2, 16, 128), bf16),
            pltpu.VMEM((3, 2, 2, 16, 2, 16, 128), bf16),
            pltpu.VMEM((2, 2, 16, 32, 128), f32),
            pltpu.VMEM((2, 2, 16, 32, 128), f32),
            pltpu.VMEM((2, 8, 32, 128), bf16),
            pltpu.VMEM((2, 16, 32, 128), bf16),
            pltpu.SemaphoreType.DMA((16,)),
            pltpu.SemaphoreType.DMA((3, 2, 2)),
            pltpu.SemaphoreType.DMA((3, 2, 2)),
            pltpu.SemaphoreType.DMA((2, 2)),
            pltpu.SemaphoreType.DMA((2, 2)),
            pltpu.SemaphoreType.DMA((2,)),
            pltpu.SemaphoreType.DMA((2,)),
            pltpu.SemaphoreType.DMA((4,)),
        ],
        compiler_params=pltpu.CompilerParams(
            collective_id=0, has_side_effects=True, vmem_limit_bytes=48 * 1024 * 1024
        ),
    )(
        field.reshape(2, 4096, 128),
        upstream.reshape(2, 4096, 128),
        mode_weights.reshape(16, 2, 256, 128),
        skip_weight,
        channel_bias.reshape(1, 128),
        *[jnp.asarray(table) for table in tables],
    )
    return out.reshape(1, 2, 64, 64, 128), grad.reshape(16, 1, 2, 2, 128, 128)


def solution(mesh):
    in_specs = (
        P("grp", "pen", None, None, None),
        P("grp", "pen", None, None, None),
        P(None, "pen", "grp", None, None, None),
        P(),
        P(),
    )
    out_specs = (P("grp", "pen", None, None, None), P(None, "pen", "grp", None, None, None))
    return jax.shard_map(
        functools.partial(shards, make_tables()), mesh=mesh, in_specs=in_specs, out_specs=out_specs, check_vma=False
    )
```

```python
import functools
import math

import jax
import jax.numpy as jnp
import ml_dtypes
import numpy as np
from jax import lax
from jax.experimental import pallas as pl
from jax.experimental.pallas import tpu as pltpu
from jax.sharding import PartitionSpec as P

MESH = pl.DeviceIdType.MESH
f32 = jnp.float32
bf16 = jnp.bfloat16


def rotation(angle, inverse):
    cosine, sine = np.cos(angle), np.sin(angle)
    sign = -1.0 if inverse else 1.0
    real_row = np.stack([cosine, sign * sine], axis=-1)
    imag_row = np.stack([-sign * sine, cosine], axis=-1)
    return np.stack([real_row, imag_row], axis=-2) / 8.0


def halves(table, axis):
    high = table.astype(ml_dtypes.bfloat16)
    low = (table - high.astype(np.float64)).astype(ml_dtypes.bfloat16)
    return np.concatenate([high, low], axis=axis)


def make_tables():
    turn = 2.0 * math.pi / 64.0
    cell = np.arange(64)
    depth = turn * (np.arange(16)[:, None] * cell[None, :] % 64)
    weight = np.where(np.arange(16) == 0, 1.0, 2.0)[:, None, None]
    depth = np.stack([np.cos(depth), -np.sin(depth)], axis=1) / 8.0
    by_parity = lambda t: t.reshape(8, 2, 2, 64).transpose(1, 0, 2, 3)
    eye = np.eye
    t1 = np.einsum("carz,yw->cayrwz", by_parity(depth), eye(4)).reshape(128, 256)
    t6 = np.einsum("carz,yw->yzcawr", by_parity(depth * weight), eye(4)).reshape(256, 128)
    ky = np.arange(16)[None, :] - 16 * np.arange(2)[:, None]
    row = turn * (ky[:, :, None] * cell % 64)
    t2 = np.einsum("hdyrs,ab->dahrbys", rotation(row, False), eye(2)).reshape(128, 256)
    t5 = np.einsum("hdyrs,ab->ayrdbhs", rotation(row, True), eye(4)).reshape(512, 256)
    kx = np.where(np.arange(16) < 8, np.arange(16), np.arange(16) - 16)
    plane = turn * (kx[:, None] * cell % 64)
    forward = rotation(plane, False).reshape(16, 2, 16, 2, 2, 2)
    backward = rotation(plane, True).reshape(16, 2, 16, 2, 2, 2)
    t3 = np.einsum("kXserv,ab,hi->Xeahkrsbiv", forward, eye(4), eye(2)).reshape(2, 2, 256, 256)
    t4 = np.einsum("kXserv,ab,hi->Xesahribkv", backward, eye(4), eye(2)).reshape(2, 2, 256, 256)
    swap = np.eye(256).reshape(8, 32, 256).transpose(1, 0, 2).reshape(256, 256)
    return (
        halves(t1, 0),
        halves(t2, 0),
        halves(t3, 2),
        halves(t4, 2),
        halves(t5, 0),
        halves(t6, 1),
        np.concatenate([swap, swap], axis=1).astype(ml_dtypes.bfloat16),
        np.ascontiguousarray(swap.T).astype(ml_dtypes.bfloat16),
    )


def dot(left, right):
    return jnp.dot(left, right, preferred_element_type=f32)


def split(values):
    high = values.astype(bf16)
    return high, (values - high.astype(f32)).astype(bf16)


def dot_split(table, values):
    rows = table.shape[0] // 2
    both = dot(table, jnp.concatenate(split(values), axis=1))
    return both[:rows, :128] + both[:rows, 128:] + both[rows:, :128]


def dot_exact(table, values):
    rows = table.shape[0] // 2
    both = dot(table, values)
    return both[:rows] + both[rows:]


SCALED = (
    0.11283793162135076,
    0.11283476245314182,
    0.10392192770562217,
    0.0842669599289443,
    0.07073040277585074,
    -0.002833797179664962,
    0.08457735964663142,
    -0.09147177273287684,
    0.025136288482206462,
)


def gelu_pair(v):
    bell = jnp.exp(-0.5 * (v * v))
    t = 1.0 / (1.0 + 0.282842712474619 * jnp.abs(v))
    series = jnp.full_like(t, SCALED[-1] * 1.0)
    for coefficient in SCALED[-2::-1]:
        series = series * t + coefficient
    tail = bell * (t * series)
    phi = jnp.where(v >= 0, 1.0 - tail, tail)
    return v * phi, phi + v * (bell * (1.0 / math.sqrt(2.0 * math.pi)))


def kernel(
    field_hbm, up_hbm, weight_hbm, skip_hbm, bias_hbm, t1_hbm, t2_hbm, t3_hbm, t4_hbm, t5_hbm, t6_hbm, gather_hbm, scatter_hbm,
    out_hbm, grad_hbm,
    field, up, weight, skip, bias, t1, t2, t3, t4, t5, t6, gather, scatter,
    base, out, grad, zbuf, ybuf, rows, pairs, mixed,
    ring_send, ring_recv, wide_send, wide_recv, back_send, back_recv,
    load_sem, ring_ssem, ring_rsem, wide_ssem, wide_rsem, back_ssem, back_rsem, store_sem,
):
    g = lax.axis_index("grp")
    p = lax.axis_index("pen")
    x_hi = p // 16
    d = lax.rem(p, 16)
    w = g * 2 + x_hi

    def ring_peer(i):
        to = lax.rem(d + 8 + (i // 2) * (2 * lax.rem(i, 2) - 1) + 16, 16)
        return to, (g, x_hi * 16 + to)

    def wide_peer(i):
        to = lax.rem(w + i, 16)
        return to, (to // 2, lax.rem(to, 2) * 16 + d)

    barrier = pltpu.get_barrier_semaphore()

    def greet(i, carry):
        for peer in (ring_peer, wide_peer):
            pl.semaphore_signal(barrier, inc=1, device_id=peer(i)[1], device_id_type=MESH)
        return carry

    lax.fori_loop(1, 16, greet, 0)

    loads = []

    def load(source, target):
        copy = pltpu.make_async_copy(source, target, load_sem.at[len(loads)])
        copy.start()
        loads.append(copy)
        return copy

    t1_load = load(t1_hbm, t1)
    quarters = [
        load(field_hbm.at[:, pl.ds(n * 1024, 1024), :], field.at[:, pl.ds(n * 1024, 1024), :]) for n in range(4)
    ]
    t2_load = load(t2_hbm, t2)
    skip_load = load(skip_hbm, skip)
    bias_load = load(bias_hbm, bias)
    t3_load = load(t3_hbm.at[x_hi], t3)
    gather_load = load(gather_hbm, gather)
    weight_load = load(weight_hbm, weight)
    scatter_load = load(scatter_hbm, scatter)
    t4_load = load(t4_hbm.at[x_hi], t4)
    t5_load = load(t5_hbm, t5)
    t6_load = load(t6_hbm, t6)
    up_load = load(up_hbm, up)

    def ring_start(n, e, c):
        source, target = ring_send.at[n, e, c], ring_recv.at[n, e, c]
        pltpu.make_async_copy(source.at[d], target.at[d], ring_rsem.at[n, e, c]).start()

        def send(i, carry):
            to, device = ring_peer(i)
            pltpu.make_async_remote_copy(
                src_ref=source.at[to],
                dst_ref=target.at[d],
                send_sem=ring_ssem.at[n, e, c],
                recv_sem=ring_rsem.at[n, e, c],
                device_id=device,
                device_id_type=MESH,
            ).start()
            return carry

        lax.fori_loop(1, 16, send, 0)

    def wide_start(n, c):
        source, target = wide_send.at[n, c], wide_recv.at[n, c]
        slot = x_hi * 8 + g
        pltpu.make_async_copy(source.at[w], target.at[slot], wide_rsem.at[n, c]).start()

        def send(i, carry):
            to, device = wide_peer(i)
            pltpu.make_async_remote_copy(
                src_ref=source.at[to],
                dst_ref=target.at[slot],
                send_sem=wide_ssem.at[n, c],
                recv_sem=wide_rsem.at[n, c],
                device_id=device,
                device_id_type=MESH,
            ).start()
            return carry

        lax.fori_loop(1, 16, send, 0)

    def back_start(c):
        source, target = back_send.at[c], back_recv.at[c]
        slot = (g // 4) * 8 + x_hi * 4 + lax.rem(g, 4)
        pltpu.make_async_copy(source.at[g], target.at[slot], back_rsem.at[c]).start()

        def send(i, carry):
            to, device = wide_peer(i)
            pltpu.make_async_remote_copy(
                src_ref=source.at[to // 2],
                dst_ref=target.at[slot],
                send_sem=back_ssem.at[c],
                recv_sem=back_rsem.at[c],
                device_id=device,
                device_id_type=MESH,
            ).start()
            return carry

        lax.fori_loop(1, 16, send, 0)

    def drain(buffer, semaphore):
        pltpu.make_async_copy(buffer, buffer, semaphore).wait()

    def depth_step(e, m, values):
        tile = dot_split(t1[...], values).reshape(16, 8, 128)
        zbuf[e, :, pl.ds(pl.multiple_of(m * 8, 8), 8), :] = tile

    def row_step(n, e, c):
        for q in range(2):
            tiles = []
            for half in range(2):
                first = c * 8 + q * 4 + half * 2
                values = zbuf[e, first : first + 2].reshape(256, 128)
                tiles.append(dot_split(t2[...], values).reshape(16, 8, 128))
            ring_send[n, e, c, :, q] = jnp.concatenate(tiles, axis=1).astype(bf16)

    def plane_step(n, c):
        for q in range(2):
            total = dot_exact(t3[0], ring_recv[n, 0, c, :, q].reshape(256, 128))
            total += dot_exact(t3[1], ring_recv[n, 1, c, :, q].reshape(256, 128))
            wide_send[n // 2, c, q * 8 : q * 8 + 8] = total.reshape(8, 32, 128)

    def collect(n, c):
        summed = (wide_recv[n, c, 0:8] + wide_recv[n, c, 8:16]).reshape(256, 128)
        rows[...] = dot(gather[...], jnp.concatenate(split(summed), axis=0))

    t1_load.wait()
    for n in range(4):
        quarters[n].wait()

        for m in range(n * 4, n * 4 + 4):
            here = pl.ds(m * 256, 256)
            high_0, low_0 = split(field[0, here, :])
            high_1, low_1 = split(field[1, here, :])
            both = dot(t1[...], jnp.concatenate([high_0, high_1], axis=1))
            tile = both[:128] + both[128:] + dot(t1[:128], jnp.concatenate([low_0, low_1], axis=1))
            for e in range(2):
                zbuf[e, :, m * 8 : m * 8 + 8, :] = tile[:, e * 128 : e * 128 + 128].reshape(16, 8, 128)
    t2_load.wait()
    for c in range(2):
        for e in range(2):
            row_step(0, e, c)
            if c == 0 and e == 0:
                pl.semaphore_wait(barrier, 30)
            ring_start(0, e, c)

    skip_load.wait()
    bias_load.wait()
    skip_row = jnp.concatenate(split(skip[...]), axis=1)
    skip_both = jnp.concatenate([skip_row, skip_row], axis=0)

    for e in range(2):

        def skip_loop(m, carry):
            for i in range(8):
                here = pl.ds(pl.multiple_of(m * 2048 + i * 256, 256), 256)
                both = dot(jnp.concatenate(split(field[e, here, :]), axis=1), skip_both)
                base[e, here, :] = both[:, :128] + both[:, 128:] + bias[...]
            return carry

        lax.fori_loop(0, 2, skip_loop, 0)

    t3_load.wait()
    for c in range(2):
        for e in range(2):
            drain(ring_recv.at[0, e, c], ring_rsem.at[0, e, c])
        plane_step(0, c)
        wide_start(0, c)

    gather_load.wait()
    weight_load.wait()
    scatter_load.wait()
    for c in range(2):
        drain(wide_recv.at[0, c], wide_rsem.at[0, c])
        collect(0, c)

        def mix_loop(m, carry):
            for i in range(4):
                k = m * 4 + i
                real = rows[pl.ds(pl.multiple_of(k * 16, 16), 8), :]
                imag = rows[pl.ds(pl.multiple_of(k * 16 + 8, 8), 8), :]
                upper = jnp.concatenate([real, -imag], axis=1)
                lower = jnp.concatenate([imag, real], axis=1)
                paired = jnp.concatenate([upper, lower], axis=0).astype(bf16)
                pairs[c, k] = paired
                mixed[pl.ds(pl.multiple_of(k * 16, 16), 16), :] = dot(paired, weight[k, c]).astype(bf16)
            return carry

        lax.fori_loop(0, 4, mix_loop, 0)
        back_send[c] = dot(scatter[...], mixed[...]).astype(bf16).reshape(8, 32, 128)
        back_start(c)

    t4_load.wait()
    for c in range(2):
        drain(back_recv.at[c], back_rsem.at[c])
        for q in range(2):
            values = back_recv[c, q * 8 : q * 8 + 8].reshape(256, 128)
            for e in range(2):
                ring_send[1, e, c, :, q] = dot_exact(t4[e], values).reshape(16, 16, 128).astype(bf16)
        ring_start(1, 0, c)
    ring_start(1, 1, 0)
    ring_start(1, 1, 1)

    t5_load.wait()
    t6_load.wait()
    up_load.wait()
    stores = []
    for e in range(2):
        for c in range(2):
            drain(ring_recv.at[1, e, c], ring_rsem.at[1, e, c])
            for q in range(2):
                first = c * 8 + q * 4
                values = ring_recv[1, e, c, :, q].reshape(256, 128)
                ybuf[first : first + 4] = dot_exact(t5[...], values).reshape(4, 128, 128)

        def cell_loop(m, carry):
            for i in range(4):
                k = m * 4 + i
                values = ybuf[:, pl.ds(pl.multiple_of(k * 8, 8), 8), :].reshape(128, 128)
                half = jnp.concatenate(split(values), axis=1)
                both = dot(t6[...], jnp.concatenate([half, half], axis=0))
                here = pl.ds(pl.multiple_of(k * 256, 256), 256)
                value, slope = gelu_pair(both[:, :128] + both[:, 128:] + base[e, here, :])
                out[e, here, :] = value.astype(bf16)
                depth_step(e, k, slope * up[e, here, :].astype(f32))
            return carry

        lax.fori_loop(0, 4, cell_loop, 0)
        store = pltpu.make_async_copy(out.at[e], out_hbm.at[e], store_sem.at[e])
        store.start()
        stores.append(store)
        for c in range(2):
            row_step(2, e, c)
            ring_start(2, e, c)

    for c in range(2):
        for e in range(2):
            drain(ring_recv.at[2, e, c], ring_rsem.at[2, e, c])
        plane_step(2, c)
        wide_start(1, c)

    for c in range(2):
        drain(wide_recv.at[1, c], wide_rsem.at[1, c])
        collect(1, c)
        scale = jnp.where(g == 0, 1.0, 2.0).astype(f32) if c == 0 else f32(2.0)

        def grad_loop(m, carry):
            for i in range(4):
                k = m * 4 + i
                cotangent = (rows[pl.ds(pl.multiple_of(k * 16, 16), 16), :] * scale).astype(bf16)
                product = lax.dot_general(
                    pairs[c, k], cotangent, (((0,), (0,)), ((), ())), preferred_element_type=f32
                )
                grad[c, k] = product.astype(bf16)
            return carry

        lax.fori_loop(0, 4, grad_loop, 0)
        store = pltpu.make_async_copy(grad.at[c], grad_hbm.at[:, c], store_sem.at[2 + c])
        store.start()
        stores.append(store)

    for n in range(3):
        for e in range(2):
            for c in range(2):
                drain(ring_send.at[n, e, c, pl.ds(0, 15)], ring_ssem.at[n, e, c])
    for n in range(2):
        for c in range(2):
            drain(wide_send.at[n, c, pl.ds(0, 15)], wide_ssem.at[n, c])
    for c in range(2):
        drain(back_recv.at[c, pl.ds(0, 15)], back_ssem.at[c])
    for store in stores:
        store.wait()


def shards(tables, field, upstream, mode_weights, skip_weight, channel_bias):
    anywhere = pl.BlockSpec(memory_space=pl.ANY)
    out, grad = pl.pallas_call(
        kernel,
        out_shape=(
            jax.ShapeDtypeStruct((2, 4096, 128), bf16),
            jax.ShapeDtypeStruct((16, 2, 256, 128), bf16),
        ),
        in_specs=[anywhere] * 13,
        out_specs=(anywhere, anywhere),
        scratch_shapes=[
            pltpu.VMEM((2, 4096, 128), f32),
            pltpu.VMEM((2, 4096, 128), bf16),
            pltpu.VMEM((16, 2, 256, 128), bf16),
            pltpu.VMEM((128, 128), f32),
            pltpu.VMEM((1, 128), f32),
            pltpu.VMEM((256, 256), bf16),
            pltpu.VMEM((256, 256), bf16),
            pltpu.VMEM((2, 512, 256), bf16),
            pltpu.VMEM((2, 512, 256), bf16),
            pltpu.VMEM((1024, 256), bf16),
            pltpu.VMEM((256, 256), bf16),
            pltpu.VMEM((256, 512), bf16),
            pltpu.VMEM((256, 256), bf16),
            pltpu.VMEM((2, 4096, 128), f32),
            pltpu.VMEM((2, 4096, 128), bf16),
            pltpu.VMEM((2, 16, 256, 128), bf16),
            pltpu.VMEM((2, 16, 128, 128), f32),
            pltpu.VMEM((16, 128, 128), f32),
            pltpu.VMEM((256, 128), f32),
            pltpu.VMEM((2, 16, 16, 256), bf16),
            pltpu.VMEM((256, 128), bf16),
            pltpu.VMEM((3, 2, 2, 16, 2, 16, 128), bf16),
            pltpu.VMEM((3, 2, 2, 16, 2, 16, 128), bf16),
            pltpu.VMEM((2, 2, 16, 32, 128), f32),
            pltpu.VMEM((2, 2, 16, 32, 128), f32),
            pltpu.VMEM((2, 8, 32, 128), bf16),
            pltpu.VMEM((2, 16, 32, 128), bf16),
            pltpu.SemaphoreType.DMA((16,)),
            pltpu.SemaphoreType.DMA((3, 2, 2)),
            pltpu.SemaphoreType.DMA((3, 2, 2)),
            pltpu.SemaphoreType.DMA((2, 2)),
            pltpu.SemaphoreType.DMA((2, 2)),
            pltpu.SemaphoreType.DMA((2,)),
            pltpu.SemaphoreType.DMA((2,)),
            pltpu.SemaphoreType.DMA((4,)),
        ],
        compiler_params=pltpu.CompilerParams(
            collective_id=0, has_side_effects=True, vmem_limit_bytes=63 * 1024 * 1024
        ),
    )(
        field.reshape(2, 4096, 128),
        upstream.reshape(2, 4096, 128),
        mode_weights.reshape(16, 2, 256, 128),
        skip_weight,
        channel_bias.reshape(1, 128),
        *[jnp.asarray(table) for table in tables],
    )
    return out.reshape(1, 2, 64, 64, 128), grad.reshape(16, 1, 2, 2, 128, 128)


def solution(mesh):
    in_specs = (
        P("grp", "pen", None, None, None),
        P("grp", "pen", None, None, None),
        P(None, "pen", "grp", None, None, None),
        P(),
        P(),
    )
    out_specs = (P("grp", "pen", None, None, None), P(None, "pen", "grp", None, None, None))
    return jax.shard_map(
        functools.partial(shards, make_tables()), mesh=mesh, in_specs=in_specs, out_specs=out_specs, check_vma=False
    )
```

```python
import functools
import math

import jax
import jax.numpy as jnp
import ml_dtypes
import numpy as np
from jax import lax
from jax.experimental import pallas as pl
from jax.experimental.pallas import tpu as pltpu
from jax.sharding import PartitionSpec as P

MESH = pl.DeviceIdType.MESH
f32 = jnp.float32
bf16 = jnp.bfloat16


def rotation(angle, inverse):
    cosine, sine = np.cos(angle), np.sin(angle)
    sign = -1.0 if inverse else 1.0
    real_row = np.stack([cosine, sign * sine], axis=-1)
    imag_row = np.stack([-sign * sine, cosine], axis=-1)
    return np.stack([real_row, imag_row], axis=-2) / 8.0


def halves(table, axis):
    high = table.astype(ml_dtypes.bfloat16)
    low = (table - high.astype(np.float64)).astype(ml_dtypes.bfloat16)
    return np.concatenate([high, low], axis=axis)


def make_tables():
    turn = 2.0 * math.pi / 64.0
    cell = np.arange(64)
    depth = turn * (np.arange(16)[:, None] * cell[None, :] % 64)
    weight = np.where(np.arange(16) == 0, 1.0, 2.0)[:, None, None]
    depth = np.stack([np.cos(depth), -np.sin(depth)], axis=1) / 8.0
    by_parity = lambda t: t.reshape(8, 2, 2, 64).transpose(1, 0, 2, 3)
    eye = np.eye
    t1 = np.einsum("carz,yw->cayrwz", by_parity(depth), eye(4)).reshape(128, 256)
    t6 = np.einsum("carz,yw->yzcawr", by_parity(depth * weight), eye(4)).reshape(256, 128)
    ky = np.arange(16)[None, :] - 16 * np.arange(2)[:, None]
    row = turn * (ky[:, :, None] * cell % 64)
    t2 = np.einsum("hdyrs,ab->dahrbys", rotation(row, False), eye(2)).reshape(128, 256)
    t5 = np.einsum("hdyrs,ab->ayrdbhs", rotation(row, True), eye(4)).reshape(512, 256)
    kx = np.where(np.arange(16) < 8, np.arange(16), np.arange(16) - 16)
    plane = turn * (kx[:, None] * cell % 64)
    forward = rotation(plane, False).reshape(16, 2, 16, 2, 2, 2)
    backward = rotation(plane, True).reshape(16, 2, 16, 2, 2, 2)
    t3 = np.einsum("kXserv,ab,hi->Xeahkrsbiv", forward, eye(4), eye(2)).reshape(2, 2, 256, 256)
    t4 = np.einsum("kXserv,ab,hi->Xesahribkv", backward, eye(4), eye(2)).reshape(2, 2, 256, 256)
    swap = np.eye(256).reshape(8, 32, 256).transpose(1, 0, 2).reshape(256, 256)
    return (
        halves(t1, 0),
        halves(t2, 0),
        halves(t3, 2),
        halves(t4, 2),
        halves(t5, 0),
        halves(t6, 1),
        np.concatenate([swap, swap], axis=1).astype(ml_dtypes.bfloat16),
        np.ascontiguousarray(swap.T).astype(ml_dtypes.bfloat16),
    )


def dot(left, right):
    return jnp.dot(left, right, preferred_element_type=f32)


def split(values):
    high = values.astype(bf16)
    return high, (values - high.astype(f32)).astype(bf16)


def dot_split(table, values):
    rows = table.shape[0] // 2
    both = dot(table, jnp.concatenate(split(values), axis=1))
    return both[:rows, :128] + both[:rows, 128:] + both[rows:, :128]


def dot_exact(table, values):
    rows = table.shape[0] // 2
    both = dot(table, values)
    return both[:rows] + both[rows:]


def gelu_pair(v):
    phi = 0.5 + 0.5 * lax.erf(v * math.sqrt(0.5))
    bell = jnp.exp2((v * v) * (-0.5 * math.log2(math.e)))
    return v * phi, phi + v * (bell * (1.0 / math.sqrt(2.0 * math.pi)))


def kernel(
    field_hbm, up_hbm, weight_hbm, skip_hbm, bias_hbm, t1_hbm, t2_hbm, t3_hbm, t4_hbm, t5_hbm, t6_hbm, gather_hbm, scatter_hbm,
    out_hbm, grad_hbm,
    field, up, weight, skip, bias, t1, t2, t3, t4, t5, t6, gather, scatter,
    base, out, grad, zbuf, ybuf, rows, pairs, mixed,
    first_send, first_recv, ring_send, ring_recv, wide_send, wide_recv, back_send, back_recv,
    load_sem, first_ssem, first_rsem, ring_ssem, ring_rsem, wide_ssem, wide_rsem, back_ssem, back_rsem, store_sem,
):
    g = lax.axis_index("grp")
    p = lax.axis_index("pen")
    x_hi = p // 16
    d = lax.rem(p, 16)
    w = g * 2 + x_hi
    half_g = g // 4

    def ring_peer(i):
        to = lax.rem(d + 8 + (i // 2) * (2 * lax.rem(i, 2) - 1) + 16, 16)
        return to, (g, x_hi * 16 + to)

    def wide_peer(i):
        to = lax.rem(w + i, 16)
        return to, (to // 2, lax.rem(to, 2) * 16 + d)

    barrier = pltpu.get_barrier_semaphore()

    def greet(i, carry):
        for peer in (ring_peer, wide_peer):
            pl.semaphore_signal(barrier, inc=1, device_id=peer(i)[1], device_id_type=MESH)
        return carry

    lax.fori_loop(1, 16, greet, 0)

    loads = []

    def load(source, target):
        copy = pltpu.make_async_copy(source, target, load_sem.at[len(loads)])
        copy.start()
        loads.append(copy)
        return copy

    t1_load = load(t1_hbm, t1)
    quarters = [
        load(field_hbm.at[:, pl.ds(n * 1024, 1024), :], field.at[:, pl.ds(n * 1024, 1024), :]) for n in range(4)
    ]
    t2_load = load(t2_hbm, t2)
    skip_load = load(skip_hbm, skip)
    bias_load = load(bias_hbm, bias)

    def ring_start(source, target, ssem, rsem):
        pltpu.make_async_copy(source.at[d], target.at[d], rsem).start()

        def send(i, carry):
            to, device = ring_peer(i)
            pltpu.make_async_remote_copy(
                src_ref=source.at[to],
                dst_ref=target.at[d],
                send_sem=ssem,
                recv_sem=rsem,
                device_id=device,
                device_id_type=MESH,
            ).start()
            return carry

        lax.fori_loop(1, 16, send, 0)

    def first_sent(c, q):
        drain(first_send.at[c, q, pl.ds(0, 15)], first_ssem.at[c, q])

    def plane_sent(n, e, c):
        drain(ring_send.at[n, e, c, pl.ds(0, 15)], ring_ssem.at[n, e, c])

    def first_start(c, q):
        ring_start(first_send.at[c, q], first_recv.at[c, q], first_ssem.at[c, q], first_rsem.at[c, q])

    def plane_start(n, e, c):
        ring_start(ring_send.at[n, e, c], ring_recv.at[n, e, c], ring_ssem.at[n, e, c], ring_rsem.at[n, e, c])

    def wide_start(n, c, q):
        source, target = wide_send.at[n, c, q], wide_recv.at[n, c]
        slot = x_hi * 8 + g
        mine = lax.rem(w, 8)

        def send(i, carry):
            to = lax.rem(mine + i, 8)
            pltpu.make_async_remote_copy(
                src_ref=source.at[to],
                dst_ref=target.at[slot],
                send_sem=wide_ssem.at[n, c, q],
                recv_sem=wide_rsem.at[n, c],
                device_id=(q * 4 + to // 2, lax.rem(to, 2) * 16 + d),
                device_id_type=MESH,
            ).start()
            return carry

        lax.fori_loop(1, 8, send, 0)

        @pl.when(half_g == q)
        def _():
            pltpu.make_async_copy(source.at[mine], target.at[slot], wide_rsem.at[n, c]).start()

        @pl.when(half_g != q)
        def _():
            send(0, 0)

    def wide_drain(n, c, q):
        sent = wide_send.at[n, c, q]

        @pl.when(half_g == q)
        def _():
            drain(sent.at[pl.ds(0, 7)], wide_ssem.at[n, c, q])

        @pl.when(half_g != q)
        def _():
            drain(sent, wide_ssem.at[n, c, q])

    def back_start(c):
        source, target = back_send.at[c], back_recv.at[c]
        slot = (g // 4) * 8 + x_hi * 4 + lax.rem(g, 4)
        pltpu.make_async_copy(source.at[g], target.at[slot], back_rsem.at[c, half_g]).start()

        def send(i, carry):
            to, device = wide_peer(i)
            pltpu.make_async_remote_copy(
                src_ref=source.at[to // 2],
                dst_ref=target.at[slot],
                send_sem=back_ssem.at[c],
                recv_sem=back_rsem.at[c, half_g],
                device_id=device,
                device_id_type=MESH,
            ).start()
            return carry

        lax.fori_loop(1, 16, send, 0)

    def drain(buffer, semaphore):
        pltpu.make_async_copy(buffer, buffer, semaphore).wait()

    def depth_step(e, m, values):
        tile = dot_split(t1[...], values).reshape(16, 8, 128)
        zbuf[e, :, pl.ds(pl.multiple_of(m * 8, 8), 8), :] = tile

    def row_step(e, c, q):
        tiles = []
        for half in range(2):
            first = c * 8 + q * 4 + half * 2
            values = zbuf[e, first : first + 2].reshape(256, 128)
            tiles.append(dot_split(t2[...], values).reshape(16, 8, 128))
        return jnp.concatenate(tiles, axis=1).astype(bf16)

    def plane_step(n, c, q, plane_0, plane_1):
        total = dot_exact(t3[0], plane_0.reshape(256, 128)) + dot_exact(t3[1], plane_1.reshape(256, 128))
        wide_send[n, c, q] = total.reshape(8, 32, 128)

    def collect(n, c):
        summed = (wide_recv[n, c, 0:8] + wide_recv[n, c, 8:16]).reshape(256, 128)
        rows[...] = dot(gather[...], jnp.concatenate(split(summed), axis=0))

    t1_load.wait()
    for n in range(4):
        quarters[n].wait()

        for m in range(n * 4, n * 4 + 4):
            here = pl.ds(m * 256, 256)
            high_0, low_0 = split(field[0, here, :])
            high_1, low_1 = split(field[1, here, :])
            both = dot(t1[...], jnp.concatenate([high_0, high_1], axis=1))
            tile = both[:128] + both[128:] + dot(t1[:128], jnp.concatenate([low_0, low_1], axis=1))
            for e in range(2):
                zbuf[e, :, m * 8 : m * 8 + 8, :] = tile[:, e * 128 : e * 128 + 128].reshape(16, 8, 128)
    t3_load = load(t3_hbm.at[x_hi], t3)
    gather_load = load(gather_hbm, gather)
    weight_load = load(weight_hbm, weight)
    scatter_load = load(scatter_hbm, scatter)
    t4_load = load(t4_hbm.at[x_hi], t4)
    t5_load = load(t5_hbm, t5)
    t6_load = load(t6_hbm, t6)
    up_load = load(up_hbm, up)
    t2_load.wait()
    for c in range(2):
        for q in range(2):
            for e in range(2):
                first_send[c, q, :, e] = row_step(e, c, q)
            if c + q == 0:
                pl.semaphore_wait(barrier, 30)
            if c == 0:
                first_start(c, q)

    skip_load.wait()
    bias_load.wait()
    skip_row = jnp.concatenate(split(skip[...]), axis=1)
    skip_both = jnp.concatenate([skip_row, skip_row], axis=0)

    for e in range(2):

        def skip_loop(m, carry):
            for i in range(8):
                here = pl.ds(pl.multiple_of(m * 2048 + i * 256, 256), 256)
                both = dot(jnp.concatenate(split(field[e, here, :]), axis=1), skip_both)
                base[e, here, :] = both[:, :128] + both[:, 128:] + bias[...]
            return carry

        lax.fori_loop(0, 2, skip_loop, 0)
        first_sent(0, e)
        first_start(1, e)

    t3_load.wait()
    for c in range(2):
        for q in range(2):
            drain(first_recv.at[c, q], first_rsem.at[c, q])
            plane_step(0, c, q, first_recv[c, q, :, 0], first_recv[c, q, :, 1])
            wide_start(0, c, q)

    gather_load.wait()
    weight_load.wait()
    scatter_load.wait()
    for c in range(2):
        drain(wide_recv.at[0, c], wide_rsem.at[0, c])
        collect(0, c)

        def mix_loop(m, carry):
            for i in range(4):
                k = m * 4 + i
                real = rows[pl.ds(pl.multiple_of(k * 16, 16), 8), :]
                imag = rows[pl.ds(pl.multiple_of(k * 16 + 8, 8), 8), :]
                upper = jnp.concatenate([real, -imag], axis=1)
                lower = jnp.concatenate([imag, real], axis=1)
                paired = jnp.concatenate([upper, lower], axis=0).astype(bf16)
                pairs[c, k] = paired
                mixed[pl.ds(pl.multiple_of(k * 16, 16), 16), :] = dot(paired, weight[k, c]).astype(bf16)
            return carry

        lax.fori_loop(0, 4, mix_loop, 0)
        back_send[c] = dot(scatter[...], mixed[...]).astype(bf16).reshape(8, 32, 128)
        back_start(c)

    t4_load.wait()
    for c in range(2):
        for q in range(2):
            drain(back_recv.at[c, pl.ds(q * 8, 8)], back_rsem.at[c, q])
            values = back_recv[c, q * 8 : q * 8 + 8].reshape(256, 128)
            for e in range(2):
                ring_send[0, e, c, :, q] = dot_exact(t4[e], values).reshape(16, 16, 128).astype(bf16)
        plane_start(0, 0, c)
        if c == 0:
            plane_start(0, 1, 0)
    plane_sent(0, 0, 1)
    plane_start(0, 1, 1)

    t5_load.wait()
    t6_load.wait()
    up_load.wait()
    stores = []
    for e in range(2):
        for c in range(2):
            drain(ring_recv.at[0, e, c], ring_rsem.at[0, e, c])
            for q in range(2):
                first = c * 8 + q * 4
                values = ring_recv[0, e, c, :, q].reshape(256, 128)
                ybuf[first : first + 4] = dot_exact(t5[...], values).reshape(4, 128, 128)

        def cell_loop(m, carry):
            for i in range(8):
                k = m * 8 + i
                values = ybuf[:, pl.ds(pl.multiple_of(k * 8, 8), 8), :].reshape(128, 128)
                half = jnp.concatenate(split(values), axis=1)
                both = dot(t6[...], jnp.concatenate([half, half], axis=0))
                here = pl.ds(pl.multiple_of(k * 256, 256), 256)
                value, slope = gelu_pair(both[:, :128] + both[:, 128:] + base[e, here, :])
                out[e, here, :] = value.astype(bf16)
                depth_step(e, k, slope * up[e, here, :].astype(f32))
            return carry

        lax.fori_loop(0, 2, cell_loop, 0)
        store = pltpu.make_async_copy(out.at[e], out_hbm.at[e], store_sem.at[e])
        store.start()
        stores.append(store)
        for c in range(2):
            for q in range(2):
                ring_send[1, e, c, :, q] = row_step(e, c, q)
            if e == 1:
                plane_sent(1, 0, c)
            plane_start(1, e, c)

    for c in range(2):
        for e in range(2):
            drain(ring_recv.at[1, e, c], ring_rsem.at[1, e, c])
        for q in range(2):
            plane_step(1, c, q, ring_recv[1, 0, c, :, q], ring_recv[1, 1, c, :, q])
            wide_start(1, c, q)

    for c in range(2):
        drain(wide_recv.at[1, c], wide_rsem.at[1, c])
        collect(1, c)
        scale = jnp.where(g == 0, 1.0, 2.0).astype(f32) if c == 0 else f32(2.0)

        def grad_loop(m, carry):
            for i in range(4):
                k = m * 4 + i
                cotangent = (rows[pl.ds(pl.multiple_of(k * 16, 16), 16), :] * scale).astype(bf16)
                product = lax.dot_general(
                    pairs[c, k], cotangent, (((0,), (0,)), ((), ())), preferred_element_type=f32
                )
                grad[c, k] = product.astype(bf16)
            return carry

        lax.fori_loop(0, 4, grad_loop, 0)
        store = pltpu.make_async_copy(grad.at[c], grad_hbm.at[:, c], store_sem.at[2 + c])
        store.start()
        stores.append(store)

    for n in range(2):
        for c in range(2):
            for q in range(2):
                wide_drain(n, c, q)
    for e, c in ((0, 0), (1, 0), (1, 1)):
        plane_sent(0, e, c)
    for c in range(2):
        plane_sent(1, 1, c)
        first_sent(1, c)
    for c in range(2):
        drain(back_recv.at[c, pl.ds(0, 15)], back_ssem.at[c])
    for store in stores:
        store.wait()


def shards(tables, field, upstream, mode_weights, skip_weight, channel_bias):
    anywhere = pl.BlockSpec(memory_space=pl.ANY)
    out, grad = pl.pallas_call(
        kernel,
        out_shape=(
            jax.ShapeDtypeStruct((2, 4096, 128), bf16),
            jax.ShapeDtypeStruct((16, 2, 256, 128), bf16),
        ),
        in_specs=[anywhere] * 13,
        out_specs=(anywhere, anywhere),
        scratch_shapes=[
            pltpu.VMEM((2, 4096, 128), f32),
            pltpu.VMEM((2, 4096, 128), bf16),
            pltpu.VMEM((16, 2, 256, 128), bf16),
            pltpu.VMEM((128, 128), f32),
            pltpu.VMEM((1, 128), f32),
            pltpu.VMEM((256, 256), bf16),
            pltpu.VMEM((256, 256), bf16),
            pltpu.VMEM((2, 512, 256), bf16),
            pltpu.VMEM((2, 512, 256), bf16),
            pltpu.VMEM((1024, 256), bf16),
            pltpu.VMEM((256, 256), bf16),
            pltpu.VMEM((256, 512), bf16),
            pltpu.VMEM((256, 256), bf16),
            pltpu.VMEM((2, 4096, 128), f32),
            pltpu.VMEM((2, 4096, 128), bf16),
            pltpu.VMEM((2, 16, 256, 128), bf16),
            pltpu.VMEM((2, 16, 128, 128), f32),
            pltpu.VMEM((16, 128, 128), f32),
            pltpu.VMEM((256, 128), f32),
            pltpu.VMEM((2, 16, 16, 256), bf16),
            pltpu.VMEM((256, 128), bf16),
            pltpu.VMEM((2, 2, 16, 2, 16, 128), bf16),
            pltpu.VMEM((2, 2, 16, 2, 16, 128), bf16),
            pltpu.VMEM((2, 2, 2, 16, 2, 16, 128), bf16),
            pltpu.VMEM((2, 2, 2, 16, 2, 16, 128), bf16),
            pltpu.VMEM((2, 2, 2, 8, 32, 128), f32),
            pltpu.VMEM((2, 2, 16, 32, 128), f32),
            pltpu.VMEM((2, 8, 32, 128), bf16),
            pltpu.VMEM((2, 16, 32, 128), bf16),
            pltpu.SemaphoreType.DMA((16,)),
            pltpu.SemaphoreType.DMA((2, 2)),
            pltpu.SemaphoreType.DMA((2, 2)),
            pltpu.SemaphoreType.DMA((2, 2, 2)),
            pltpu.SemaphoreType.DMA((2, 2, 2)),
            pltpu.SemaphoreType.DMA((2, 2, 2)),
            pltpu.SemaphoreType.DMA((2, 2)),
            pltpu.SemaphoreType.DMA((2,)),
            pltpu.SemaphoreType.DMA((2, 2)),
            pltpu.SemaphoreType.DMA((4,)),
        ],
        compiler_params=pltpu.CompilerParams(
            collective_id=0, has_side_effects=True, vmem_limit_bytes=63 * 1024 * 1024
        ),
    )(
        field.reshape(2, 4096, 128),
        upstream.reshape(2, 4096, 128),
        mode_weights.reshape(16, 2, 256, 128),
        skip_weight,
        channel_bias.reshape(1, 128),
        *[jnp.asarray(table) for table in tables],
    )
    return out.reshape(1, 2, 64, 64, 128), grad.reshape(16, 1, 2, 2, 128, 128)


def solution(mesh):
    in_specs = (
        P("grp", "pen", None, None, None),
        P("grp", "pen", None, None, None),
        P(None, "pen", "grp", None, None, None),
        P(),
        P(),
    )
    out_specs = (P("grp", "pen", None, None, None), P(None, "pen", "grp", None, None, None))
    return jax.shard_map(
        functools.partial(shards, make_tables()), mesh=mesh, in_specs=in_specs, out_specs=out_specs, check_vma=False
    )
```

```python
import functools
import math

import jax
import jax.numpy as jnp
import ml_dtypes
import numpy as np
from jax import lax
from jax.experimental import pallas as pl
from jax.experimental.pallas import tpu as pltpu
from jax.sharding import PartitionSpec as P

MESH = pl.DeviceIdType.MESH
f32 = jnp.float32
bf16 = jnp.bfloat16


def rotation(angle, inverse):
    cosine, sine = np.cos(angle), np.sin(angle)
    sign = -1.0 if inverse else 1.0
    real_row = np.stack([cosine, sign * sine], axis=-1)
    imag_row = np.stack([-sign * sine, cosine], axis=-1)
    return np.stack([real_row, imag_row], axis=-2) / 8.0


def halves(table, axis):
    high = table.astype(ml_dtypes.bfloat16)
    low = (table - high.astype(np.float64)).astype(ml_dtypes.bfloat16)
    return np.concatenate([high, low], axis=axis)


def make_tables():
    turn = 2.0 * math.pi / 64.0
    cell = np.arange(64)
    depth = turn * (np.arange(16)[:, None] * cell[None, :] % 64)
    weight = np.where(np.arange(16) == 0, 1.0, 2.0)[:, None, None]
    depth = np.stack([np.cos(depth), -np.sin(depth)], axis=1) / 8.0
    by_parity = lambda t: t.reshape(8, 2, 2, 64).transpose(1, 0, 2, 3)
    eye = np.eye
    t1 = np.einsum("carz,yw->cayrwz", by_parity(depth), eye(4)).reshape(128, 256)
    t6 = np.einsum("carz,yw->yzcawr", by_parity(depth * weight), eye(4)).reshape(256, 128)
    ky = np.arange(16)[None, :] - 16 * np.arange(2)[:, None]
    row = turn * (ky[:, :, None] * cell % 64)
    t2 = np.einsum("hdyrs,ab->dahrbys", rotation(row, False), eye(2)).reshape(128, 256)
    t5 = np.einsum("hdyrs,ab->ayrdbhs", rotation(row, True), eye(4)).reshape(512, 256)
    kx = np.where(np.arange(16) < 8, np.arange(16), np.arange(16) - 16)
    plane = turn * (kx[:, None] * cell % 64)
    forward = rotation(plane, False).reshape(16, 2, 16, 2, 2, 2)
    backward = rotation(plane, True).reshape(16, 2, 16, 2, 2, 2)
    t3 = np.einsum("kXserv,ab,hi->Xeahkrsbiv", forward, eye(4), eye(2)).reshape(2, 2, 256, 256)
    t4 = np.einsum("kXserv,ab,hi->Xesahribkv", backward, eye(4), eye(2)).reshape(2, 2, 256, 256)
    swap = np.eye(256).reshape(8, 32, 256).transpose(1, 0, 2).reshape(256, 256)
    return (
        halves(t1, 0),
        halves(t2, 0),
        halves(t3, 2),
        halves(t4, 2),
        halves(t5, 0),
        halves(t6, 1),
        np.concatenate([swap, swap], axis=1).astype(ml_dtypes.bfloat16),
        np.ascontiguousarray(swap.T).astype(ml_dtypes.bfloat16),
    )


def dot(left, right):
    return jnp.dot(left, right, preferred_element_type=f32)


def split(values):
    high = values.astype(bf16)
    return high, (values - high.astype(f32)).astype(bf16)


def dot_split(table, values):
    rows = table.shape[0] // 2
    both = dot(table, jnp.concatenate(split(values), axis=1))
    return both[:rows, :128] + both[:rows, 128:] + both[rows:, :128]


def dot_exact(table, values):
    rows = table.shape[0] // 2
    both = dot(table, values)
    return both[:rows] + both[rows:]


def gelu_pair(v):
    phi = 0.5 + 0.5 * lax.erf(v * math.sqrt(0.5))
    bell = jnp.exp2((v * v) * (-0.5 * math.log2(math.e)))
    return v * phi, phi + v * (bell * (1.0 / math.sqrt(2.0 * math.pi)))


def kernel(
    field_hbm, up_hbm, weight_hbm, skip_hbm, bias_hbm, t1_hbm, t2_hbm, t3_hbm, t4_hbm, t5_hbm, t6_hbm, gather_hbm, scatter_hbm,
    out_hbm, grad_hbm,
    field, up, weight, skip, bias, t1, t2, t3, t4, t5, t6, gather, scatter,
    base, out, grad, zbuf, ybuf, rows, pairs, mixed,
    first_send, first_recv, ring_send, ring_recv, wide_send, wide_recv, back_send, back_recv,
    load_sem, first_ssem, first_rsem, ring_ssem, ring_rsem, wide_ssem, wide_rsem, back_ssem, back_rsem, store_sem,
):
    g = lax.axis_index("grp")
    p = lax.axis_index("pen")
    x_hi = p // 16
    d = lax.rem(p, 16)
    w = g * 2 + x_hi
    half_g = g // 4

    def ring_peer(i):
        to = lax.rem(d + 8 + (i // 2) * (2 * lax.rem(i, 2) - 1) + 16, 16)
        return to, (g, x_hi * 16 + to)

    def wide_peer(i):
        to = lax.rem(w + i, 16)
        return to, (to // 2, lax.rem(to, 2) * 16 + d)

    barrier = pltpu.get_barrier_semaphore()

    loads = []

    def load(source, target):
        copy = pltpu.make_async_copy(source, target, load_sem.at[len(loads)])
        copy.start()
        loads.append(copy)
        return copy

    t1_load = load(t1_hbm, t1)
    pieces = [
        load(field_hbm.at[:, pl.ds(n * 512, 512), :], field.at[:, pl.ds(n * 512, 512), :]) for n in range(8)
    ]
    t2_load = load(t2_hbm, t2)
    def greet(i, carry):
        for peer in (ring_peer, wide_peer):
            pl.semaphore_signal(barrier, inc=1, device_id=peer(i)[1], device_id_type=MESH)
        return carry

    lax.fori_loop(1, 16, greet, 0)
    skip_load = load(skip_hbm, skip)
    bias_load = load(bias_hbm, bias)

    def ring_start(source, target, ssem, rsem):
        pltpu.make_async_copy(source.at[d], target.at[d], rsem).start()

        def send(i, carry):
            to, device = ring_peer(i)
            pltpu.make_async_remote_copy(
                src_ref=source.at[to],
                dst_ref=target.at[d],
                send_sem=ssem,
                recv_sem=rsem,
                device_id=device,
                device_id_type=MESH,
            ).start()
            return carry

        lax.fori_loop(1, 16, send, 0)

    def first_sent(c, q):
        drain(first_send.at[c, q, pl.ds(0, 15)], first_ssem.at[c, q])

    def plane_sent(n, e, c):
        drain(ring_send.at[n, e, c, pl.ds(0, 15)], ring_ssem.at[n, e, c])

    def first_start(c, q):
        ring_start(first_send.at[c, q], first_recv.at[c, q], first_ssem.at[c, q], first_rsem.at[c, q])

    def plane_start(n, e, c):
        ring_start(ring_send.at[n, e, c], ring_recv.at[n, e, c], ring_ssem.at[n, e, c], ring_rsem.at[n, e, c])

    def wide_start(n, c, q):
        source, target = wide_send.at[n, c, q], wide_recv.at[n, c]
        slot = x_hi * 8 + g
        mine = lax.rem(w, 8)

        def send(i, carry):
            to = lax.rem(mine + i, 8)
            pltpu.make_async_remote_copy(
                src_ref=source.at[to],
                dst_ref=target.at[slot],
                send_sem=wide_ssem.at[n, c, q],
                recv_sem=wide_rsem.at[n, c],
                device_id=(q * 4 + to // 2, lax.rem(to, 2) * 16 + d),
                device_id_type=MESH,
            ).start()
            return carry

        lax.fori_loop(1, 8, send, 0)

        @pl.when(half_g == q)
        def _():
            pltpu.make_async_copy(source.at[mine], target.at[slot], wide_rsem.at[n, c]).start()

        @pl.when(half_g != q)
        def _():
            send(0, 0)

    def wide_drain(n, c, q):
        sent = wide_send.at[n, c, q]

        @pl.when(half_g == q)
        def _():
            drain(sent.at[pl.ds(0, 7)], wide_ssem.at[n, c, q])

        @pl.when(half_g != q)
        def _():
            drain(sent, wide_ssem.at[n, c, q])

    def back_start(c):
        source, target = back_send.at[c], back_recv.at[c]
        slot = (g // 4) * 8 + x_hi * 4 + lax.rem(g, 4)
        pltpu.make_async_copy(source.at[g], target.at[slot], back_rsem.at[c, half_g]).start()

        def send(i, carry):
            to, device = wide_peer(i)
            pltpu.make_async_remote_copy(
                src_ref=source.at[to // 2],
                dst_ref=target.at[slot],
                send_sem=back_ssem.at[c],
                recv_sem=back_rsem.at[c, half_g],
                device_id=device,
                device_id_type=MESH,
            ).start()
            return carry

        lax.fori_loop(1, 16, send, 0)

    def drain(buffer, semaphore):
        pltpu.make_async_copy(buffer, buffer, semaphore).wait()

    def depth_step(e, m, values):
        tile = dot_split(t1[...], values).reshape(16, 8, 128)
        zbuf[e, :, pl.ds(pl.multiple_of(m * 8, 8), 8), :] = tile

    def row_step(e, c, q):
        tiles = []
        for half in range(2):
            first = c * 8 + q * 4 + half * 2
            values = zbuf[e, first : first + 2].reshape(256, 128)
            tiles.append(dot_split(t2[...], values).reshape(16, 8, 128))
        return jnp.concatenate(tiles, axis=1).astype(bf16)

    def plane_step(n, c, q, plane_0, plane_1):
        total = dot_exact(t3[0], plane_0.reshape(256, 128)) + dot_exact(t3[1], plane_1.reshape(256, 128))
        wide_send[n, c, q] = total.reshape(8, 32, 128)

    def collect(n, c):
        summed = (wide_recv[n, c, 0:8] + wide_recv[n, c, 8:16]).reshape(256, 128)
        rows[...] = dot(gather[...], jnp.concatenate(split(summed), axis=0))

    t1_load.wait()
    for n in range(8):
        pieces[n].wait()

        for m in range(n * 2, n * 2 + 2):
            here = pl.ds(m * 256, 256)
            high_0, low_0 = split(field[0, here, :])
            high_1, low_1 = split(field[1, here, :])
            both = dot(t1[...], jnp.concatenate([high_0, high_1], axis=1))
            tile = both[:128] + both[128:] + dot(t1[:128], jnp.concatenate([low_0, low_1], axis=1))
            for e in range(2):
                zbuf[e, :, m * 8 : m * 8 + 8, :] = tile[:, e * 128 : e * 128 + 128].reshape(16, 8, 128)
    t3_load = load(t3_hbm.at[x_hi], t3)
    gather_load = load(gather_hbm, gather)
    weight_load = load(weight_hbm, weight)
    scatter_load = load(scatter_hbm, scatter)
    t4_load = load(t4_hbm.at[x_hi], t4)
    t5_load = load(t5_hbm, t5)
    t6_load = load(t6_hbm, t6)
    up_load = load(up_hbm, up)
    t2_load.wait()
    for c in range(2):
        for q in range(2):
            for e in range(2):
                first_send[c, q, :, e] = row_step(e, c, q)
            if c + q == 0:
                pl.semaphore_wait(barrier, 30)
            if c == 0:
                first_start(c, q)

    skip_load.wait()
    bias_load.wait()
    skip_row = jnp.concatenate(split(skip[...]), axis=1)
    skip_both = jnp.concatenate([skip_row, skip_row], axis=0)

    for e in range(2):

        def skip_loop(m, carry):
            for i in range(8):
                here = pl.ds(pl.multiple_of(m * 2048 + i * 256, 256), 256)
                both = dot(jnp.concatenate(split(field[e, here, :]), axis=1), skip_both)
                base[e, here, :] = both[:, :128] + both[:, 128:] + bias[...]
            return carry

        lax.fori_loop(0, 2, skip_loop, 0)
        first_sent(0, e)
        first_start(1, e)

    t3_load.wait()
    for c in range(2):
        for q in range(2):
            drain(first_recv.at[c, q], first_rsem.at[c, q])
            plane_step(0, c, q, first_recv[c, q, :, 0], first_recv[c, q, :, 1])
            wide_start(0, c, q)

    gather_load.wait()
    weight_load.wait()
    scatter_load.wait()
    for c in range(2):
        drain(wide_recv.at[0, c], wide_rsem.at[0, c])
        collect(0, c)

        def mix_loop(m, carry):
            for i in range(8):
                k = m * 8 + i
                real = rows[pl.ds(pl.multiple_of(k * 16, 16), 8), :]
                imag = rows[pl.ds(pl.multiple_of(k * 16 + 8, 8), 8), :]
                upper = jnp.concatenate([real, -imag], axis=1)
                lower = jnp.concatenate([imag, real], axis=1)
                paired = jnp.concatenate([upper, lower], axis=0).astype(bf16)
                pairs[c, k] = paired
                mixed[pl.ds(pl.multiple_of(k * 16, 16), 16), :] = dot(paired, weight[k, c]).astype(bf16)
            return carry

        lax.fori_loop(0, 2, mix_loop, 0)
        back_send[c] = dot(scatter[...], mixed[...]).astype(bf16).reshape(8, 32, 128)
        back_start(c)

    t4_load.wait()
    for c in range(2):
        for q in range(2):
            drain(back_recv.at[c, pl.ds(q * 8, 8)], back_rsem.at[c, q])
            values = back_recv[c, q * 8 : q * 8 + 8].reshape(256, 128)
            for e in range(2):
                ring_send[0, e, c, :, q] = dot_exact(t4[e], values).reshape(16, 16, 128).astype(bf16)
        plane_start(0, 0, c)
    plane_start(0, 1, 0)
    plane_sent(0, 0, 1)
    plane_start(0, 1, 1)

    t5_load.wait()
    t6_load.wait()
    up_load.wait()
    stores = []
    for e in range(2):
        for c in range(2):
            drain(ring_recv.at[0, e, c], ring_rsem.at[0, e, c])
            for q in range(2):
                first = c * 8 + q * 4
                values = ring_recv[0, e, c, :, q].reshape(256, 128)
                ybuf[first : first + 4] = dot_exact(t5[...], values).reshape(4, 128, 128)

        def cell_loop(m, carry):
            for i in range(8):
                k = m * 8 + i
                values = ybuf[:, pl.ds(pl.multiple_of(k * 8, 8), 8), :].reshape(128, 128)
                half = jnp.concatenate(split(values), axis=1)
                both = dot(t6[...], jnp.concatenate([half, half], axis=0))
                here = pl.ds(pl.multiple_of(k * 256, 256), 256)
                value, slope = gelu_pair(both[:, :128] + both[:, 128:] + base[e, here, :])
                out[e, here, :] = value.astype(bf16)
                depth_step(e, k, slope * up[e, here, :].astype(f32))
            return carry

        lax.fori_loop(0, 2, cell_loop, 0)
        store = pltpu.make_async_copy(out.at[e], out_hbm.at[e], store_sem.at[e])
        store.start()
        stores.append(store)
        for c in range(2):
            for q in range(2):
                ring_send[1, e, c, :, q] = row_step(e, c, q)
            if e == 1 and c == 0:
                plane_sent(1, 0, 0)
            if e == 1 and c == 1:
                plane_sent(1, 0, 1)
                plane_sent(1, 1, 0)
            plane_start(1, e, c)

    for c in range(2):
        for e in range(2):
            drain(ring_recv.at[1, e, c], ring_rsem.at[1, e, c])
        for q in range(2):
            plane_step(1, c, q, ring_recv[1, 0, c, :, q], ring_recv[1, 1, c, :, q])
            wide_start(1, c, q)

    for c in range(2):
        drain(wide_recv.at[1, c], wide_rsem.at[1, c])
        collect(1, c)
        scale = jnp.where(g == 0, 1.0, 2.0).astype(f32) if c == 0 else f32(2.0)

        for half in range(2):
            for k in range(half * 8, half * 8 + 8):
                cotangent = (rows[k * 16 : k * 16 + 16, :] * scale).astype(bf16)
                product = lax.dot_general(
                    pairs[c, k], cotangent, (((0,), (0,)), ((), ())), preferred_element_type=f32
                )
                grad[c, k] = product.astype(bf16)
            part = pl.ds(half * 8, 8)
            store = pltpu.make_async_copy(grad.at[c, part], grad_hbm.at[part, c], store_sem.at[2 + 2 * c + half])
            store.start()
            stores.append(store)

    for n in range(2):
        for c in range(2):
            for q in range(2):
                wide_drain(n, c, q)
    for e, c in ((0, 0), (1, 0), (1, 1)):
        plane_sent(0, e, c)
    for c in range(2):
        first_sent(1, c)
    plane_sent(1, 1, 1)
    for c in range(2):
        drain(back_recv.at[c, pl.ds(0, 15)], back_ssem.at[c])
    for store in stores:
        store.wait()


def shards(tables, field, upstream, mode_weights, skip_weight, channel_bias):
    anywhere = pl.BlockSpec(memory_space=pl.ANY)
    out, grad = pl.pallas_call(
        kernel,
        out_shape=(
            jax.ShapeDtypeStruct((2, 4096, 128), bf16),
            jax.ShapeDtypeStruct((16, 2, 256, 128), bf16),
        ),
        in_specs=[anywhere] * 13,
        out_specs=(anywhere, anywhere),
        scratch_shapes=[
            pltpu.VMEM((2, 4096, 128), f32),
            pltpu.VMEM((2, 4096, 128), bf16),
            pltpu.VMEM((16, 2, 256, 128), bf16),
            pltpu.VMEM((128, 128), f32),
            pltpu.VMEM((1, 128), f32),
            pltpu.VMEM((256, 256), bf16),
            pltpu.VMEM((256, 256), bf16),
            pltpu.VMEM((2, 512, 256), bf16),
            pltpu.VMEM((2, 512, 256), bf16),
            pltpu.VMEM((1024, 256), bf16),
            pltpu.VMEM((256, 256), bf16),
            pltpu.VMEM((256, 512), bf16),
            pltpu.VMEM((256, 256), bf16),
            pltpu.VMEM((2, 4096, 128), f32),
            pltpu.VMEM((2, 4096, 128), bf16),
            pltpu.VMEM((2, 16, 256, 128), bf16),
            pltpu.VMEM((2, 16, 128, 128), f32),
            pltpu.VMEM((16, 128, 128), f32),
            pltpu.VMEM((256, 128), f32),
            pltpu.VMEM((2, 16, 16, 256), bf16),
            pltpu.VMEM((256, 128), bf16),
            pltpu.VMEM((2, 2, 16, 2, 16, 128), bf16),
            pltpu.VMEM((2, 2, 16, 2, 16, 128), bf16),
            pltpu.VMEM((2, 2, 2, 16, 2, 16, 128), bf16),
            pltpu.VMEM((2, 2, 2, 16, 2, 16, 128), bf16),
            pltpu.VMEM((2, 2, 2, 8, 32, 128), f32),
            pltpu.VMEM((2, 2, 16, 32, 128), f32),
            pltpu.VMEM((2, 8, 32, 128), bf16),
            pltpu.VMEM((2, 16, 32, 128), bf16),
            pltpu.SemaphoreType.DMA((20,)),
            pltpu.SemaphoreType.DMA((2, 2)),
            pltpu.SemaphoreType.DMA((2, 2)),
            pltpu.SemaphoreType.DMA((2, 2, 2)),
            pltpu.SemaphoreType.DMA((2, 2, 2)),
            pltpu.SemaphoreType.DMA((2, 2, 2)),
            pltpu.SemaphoreType.DMA((2, 2)),
            pltpu.SemaphoreType.DMA((2,)),
            pltpu.SemaphoreType.DMA((2, 2)),
            pltpu.SemaphoreType.DMA((6,)),
        ],
        compiler_params=pltpu.CompilerParams(
            collective_id=0, has_side_effects=True, vmem_limit_bytes=63 * 1024 * 1024
        ),
    )(
        field.reshape(2, 4096, 128),
        upstream.reshape(2, 4096, 128),
        mode_weights.reshape(16, 2, 256, 128),
        skip_weight,
        channel_bias.reshape(1, 128),
        *[jnp.asarray(table) for table in tables],
    )
    return out.reshape(1, 2, 64, 64, 128), grad.reshape(16, 1, 2, 2, 128, 128)


def solution(mesh):
    in_specs = (
        P("grp", "pen", None, None, None),
        P("grp", "pen", None, None, None),
        P(None, "pen", "grp", None, None, None),
        P(),
        P(),
    )
    out_specs = (P("grp", "pen", None, None, None), P(None, "pen", "grp", None, None, None))
    return jax.shard_map(
        functools.partial(shards, make_tables()), mesh=mesh, in_specs=in_specs, out_specs=out_specs, check_vma=False
    )
```

```python
import functools
import math

import jax
import jax.numpy as jnp
import ml_dtypes
import numpy as np
from jax import lax
from jax.experimental import pallas as pl
from jax.experimental.pallas import tpu as pltpu
from jax.sharding import PartitionSpec as P

MESH = pl.DeviceIdType.MESH
f32 = jnp.float32
bf16 = jnp.bfloat16


def rotation(angle, inverse):
    cosine, sine = np.cos(angle), np.sin(angle)
    sign = -1.0 if inverse else 1.0
    real_row = np.stack([cosine, sign * sine], axis=-1)
    imag_row = np.stack([-sign * sine, cosine], axis=-1)
    return np.stack([real_row, imag_row], axis=-2) / 8.0


def halves(table, axis):
    high = table.astype(ml_dtypes.bfloat16)
    low = (table - high.astype(np.float64)).astype(ml_dtypes.bfloat16)
    return np.concatenate([high, low], axis=axis)


def make_tables():
    turn = 2.0 * math.pi / 64.0
    cell = np.arange(64)
    depth = turn * (np.arange(16)[:, None] * cell[None, :] % 64)
    weight = np.where(np.arange(16) == 0, 1.0, 2.0)[:, None, None]
    depth = np.stack([np.cos(depth), -np.sin(depth)], axis=1) / 8.0
    by_parity = lambda t: t.reshape(8, 2, 2, 64).transpose(1, 0, 2, 3)
    eye = np.eye
    t1 = np.einsum("carz,yw->cayrwz", by_parity(depth), eye(4)).reshape(128, 256)
    t6 = np.einsum("carz,yw->yzcawr", by_parity(depth * weight), eye(4)).reshape(256, 128)
    ky = np.arange(16)[None, :] - 16 * np.arange(2)[:, None]
    row = turn * (ky[:, :, None] * cell % 64)
    t2 = np.einsum("hdyrs,ab->dahrbys", rotation(row, False), eye(2)).reshape(128, 256)
    t5 = np.einsum("hdyrs,ab->ayrdbhs", rotation(row, True), eye(4)).reshape(512, 256)
    kx = np.where(np.arange(16) < 8, np.arange(16), np.arange(16) - 16)
    plane = turn * (kx[:, None] * cell % 64)
    forward = rotation(plane, False).reshape(16, 2, 16, 2, 2, 2)
    backward = rotation(plane, True).reshape(16, 2, 16, 2, 2, 2)
    t3 = np.einsum("kXserv,ab,hi->Xeahkrsbiv", forward, eye(4), eye(2)).reshape(2, 2, 256, 256)
    t4 = np.einsum("kXserv,ab,hi->Xesahribkv", backward, eye(4), eye(2)).reshape(2, 2, 256, 256)
    swap = np.eye(256).reshape(8, 32, 256).transpose(1, 0, 2).reshape(256, 256)
    return (
        halves(t1, 0),
        halves(t2, 0),
        halves(t3, 2),
        halves(t4, 2),
        halves(t5, 0),
        halves(t6, 1),
        np.concatenate([swap, swap], axis=1).astype(ml_dtypes.bfloat16),
        np.ascontiguousarray(swap.T).astype(ml_dtypes.bfloat16),
    )


def dot(left, right):
    return jnp.dot(left, right, preferred_element_type=f32)


def split(values):
    high = values.astype(bf16)
    return high, (values - high.astype(f32)).astype(bf16)


def dot_split(table, values):
    rows = table.shape[0] // 2
    both = dot(table, jnp.concatenate(split(values), axis=1))
    return both[:rows, :128] + both[:rows, 128:] + both[rows:, :128]


def dot_exact(table, values):
    rows = table.shape[0] // 2
    both = dot(table, values)
    return both[:rows] + both[rows:]


def gelu_pair(v):
    phi = 0.5 + 0.5 * lax.erf(v * math.sqrt(0.5))
    bell = jnp.exp2((v * v) * (-0.5 * math.log2(math.e)))
    return v * phi, phi + v * (bell * (1.0 / math.sqrt(2.0 * math.pi)))


def kernel(
    field_hbm, up_hbm, weight_hbm, skip_hbm, bias_hbm, t1_hbm, t2_hbm, t3_hbm, t4_hbm, t5_hbm, t6_hbm, gather_hbm, scatter_hbm,
    out_hbm, grad_hbm,
    field, up, weight, skip, bias, t1, t2, t3, t4, t5, t6, gather, scatter,
    base, out, grad, zbuf, ybuf, rows, pairs, mixed,
    first_send, first_recv, ring_send, ring_recv, wide_send, wide_recv, back_send, back_recv,
    load_sem, first_ssem, first_rsem, ring_ssem, ring_rsem, wide_ssem, wide_rsem, back_ssem, back_rsem, store_sem,
):
    g = lax.axis_index("grp")
    p = lax.axis_index("pen")
    x_hi = p // 16
    d = lax.rem(p, 16)
    w = g * 2 + x_hi
    half_g = g // 4

    def ring_peer(i):
        to = lax.rem(d + 8 + (i // 2) * (2 * lax.rem(i, 2) - 1) + 16, 16)
        return to, (g, x_hi * 16 + to)

    def wide_peer(i):
        to = lax.rem(w + i, 16)
        return to, (to // 2, lax.rem(to, 2) * 16 + d)

    barrier = pltpu.get_barrier_semaphore()

    loads = []

    def load(source, target):
        copy = pltpu.make_async_copy(source, target, load_sem.at[len(loads)])
        copy.start()
        loads.append(copy)
        return copy

    t1_load = load(t1_hbm, t1)
    pieces = [
        load(field_hbm.at[:, pl.ds(n * 512, 512), :], field.at[:, pl.ds(n * 512, 512), :]) for n in range(8)
    ]
    t2_load = load(t2_hbm, t2)
    def greet(i, carry):
        for peer in (ring_peer, wide_peer):
            pl.semaphore_signal(barrier, inc=1, device_id=peer(i)[1], device_id_type=MESH)
        return carry

    lax.fori_loop(1, 16, greet, 0)
    skip_load = load(skip_hbm, skip)
    bias_load = load(bias_hbm, bias)

    def ring_start(source, target, ssem, rsem):
        pltpu.make_async_copy(source.at[d], target.at[d], rsem).start()

        def send(i, carry):
            to, device = ring_peer(i)
            pltpu.make_async_remote_copy(
                src_ref=source.at[to],
                dst_ref=target.at[d],
                send_sem=ssem,
                recv_sem=rsem,
                device_id=device,
                device_id_type=MESH,
            ).start()
            return carry

        lax.fori_loop(1, 16, send, 0)

    def first_sent(c, q):
        drain(first_send.at[c, q, pl.ds(0, 15)], first_ssem.at[c, q])

    def plane_sent(n, e, c):
        drain(ring_send.at[n, e, c, pl.ds(0, 15)], ring_ssem.at[n, e, c])

    def first_start(c, q):
        ring_start(first_send.at[c, q], first_recv.at[c, q], first_ssem.at[c, q], first_rsem.at[c, q])

    def plane_start(n, e, c):
        ring_start(ring_send.at[n, e, c], ring_recv.at[n, e, c], ring_ssem.at[n, e, c], ring_rsem.at[n, e, c])

    def wide_start(n, c, q):
        source, target = wide_send.at[n, c, q], wide_recv.at[n, c]
        slot = x_hi * 8 + g
        mine = lax.rem(w, 8)

        def send(i, carry):
            to = lax.rem(mine + i, 8)
            pltpu.make_async_remote_copy(
                src_ref=source.at[to],
                dst_ref=target.at[slot],
                send_sem=wide_ssem.at[n, c, q],
                recv_sem=wide_rsem.at[n, c],
                device_id=(q * 4 + to // 2, lax.rem(to, 2) * 16 + d),
                device_id_type=MESH,
            ).start()
            return carry

        lax.fori_loop(1, 8, send, 0)

        @pl.when(half_g == q)
        def _():
            pltpu.make_async_copy(source.at[mine], target.at[slot], wide_rsem.at[n, c]).start()

        @pl.when(half_g != q)
        def _():
            send(0, 0)

    def wide_drain(n, c, q):
        sent = wide_send.at[n, c, q]

        @pl.when(half_g == q)
        def _():
            drain(sent.at[pl.ds(0, 7)], wide_ssem.at[n, c, q])

        @pl.when(half_g != q)
        def _():
            drain(sent, wide_ssem.at[n, c, q])

    def back_start(c):
        source, target = back_send.at[c], back_recv.at[c]
        slot = (g // 4) * 8 + x_hi * 4 + lax.rem(g, 4)
        pltpu.make_async_copy(source.at[g], target.at[slot], back_rsem.at[c, half_g]).start()

        def send(i, carry):
            to, device = wide_peer(i)
            pltpu.make_async_remote_copy(
                src_ref=source.at[to // 2],
                dst_ref=target.at[slot],
                send_sem=back_ssem.at[c],
                recv_sem=back_rsem.at[c, half_g],
                device_id=device,
                device_id_type=MESH,
            ).start()
            return carry

        lax.fori_loop(1, 16, send, 0)

    def drain(buffer, semaphore):
        pltpu.make_async_copy(buffer, buffer, semaphore).wait()

    def depth_step(e, m, values):
        tile = dot_split(t1[...], values).reshape(16, 8, 128)
        zbuf[e, :, pl.ds(pl.multiple_of(m * 8, 8), 8), :] = tile

    def row_step(e, c, q):
        tiles = []
        for half in range(2):
            first = c * 8 + q * 4 + half * 2
            values = zbuf[e, first : first + 2].reshape(256, 128)
            tiles.append(dot_split(t2[...], values).reshape(16, 8, 128))
        return jnp.concatenate(tiles, axis=1).astype(bf16)

    def plane_step(n, c, q, plane_0, plane_1):
        total = dot_exact(t3[0], plane_0.reshape(256, 128)) + dot_exact(t3[1], plane_1.reshape(256, 128))
        wide_send[n, c, q] = total.reshape(8, 32, 128)

    def collect(n, c):
        summed = (wide_recv[n, c, 0:8] + wide_recv[n, c, 8:16]).reshape(256, 128)
        rows[...] = dot(gather[...], jnp.concatenate(split(summed), axis=0))

    t1_load.wait()
    for n in range(8):
        pieces[n].wait()

        for m in range(n * 2, n * 2 + 2):
            here = pl.ds(m * 256, 256)
            high_0, low_0 = split(field[0, here, :])
            high_1, low_1 = split(field[1, here, :])
            both = dot(t1[...], jnp.concatenate([high_0, high_1], axis=1))
            tile = both[:128] + both[128:] + dot(t1[:128], jnp.concatenate([low_0, low_1], axis=1))
            for e in range(2):
                zbuf[e, :, m * 8 : m * 8 + 8, :] = tile[:, e * 128 : e * 128 + 128].reshape(16, 8, 128)
    t3_load = load(t3_hbm.at[x_hi], t3)
    gather_load = load(gather_hbm, gather)
    weight_load = load(weight_hbm, weight)
    scatter_load = load(scatter_hbm, scatter)
    t4_load = load(t4_hbm.at[x_hi], t4)
    t5_load = load(t5_hbm, t5)
    t6_load = load(t6_hbm, t6)
    up_load = load(up_hbm, up)
    t2_load.wait()
    for c in range(2):
        for q in range(2):
            for e in range(2):
                first_send[c, q, :, e] = row_step(e, c, q)
            if c + q == 0:
                pl.semaphore_wait(barrier, 30)
            if c == 0:
                first_start(c, q)

    skip_load.wait()
    bias_load.wait()
    skip_row = jnp.concatenate(split(skip[...]), axis=1)
    skip_both = jnp.concatenate([skip_row, skip_row], axis=0)

    for e in range(2):

        def skip_loop(m, carry):
            for i in range(8):
                here = pl.ds(pl.multiple_of(m * 2048 + i * 256, 256), 256)
                both = dot(jnp.concatenate(split(field[e, here, :]), axis=1), skip_both)
                base[e, here, :] = both[:, :128] + both[:, 128:] + bias[...]
            return carry

        lax.fori_loop(0, 2, skip_loop, 0)
        first_sent(0, e)
        first_start(1, e)

    t3_load.wait()
    for c in range(2):
        for q in range(2):
            drain(first_recv.at[c, q], first_rsem.at[c, q])
            plane_step(0, c, q, first_recv[c, q, :, 0], first_recv[c, q, :, 1])
            wide_start(0, c, q)

    gather_load.wait()
    weight_load.wait()
    scatter_load.wait()
    for c in range(2):
        drain(wide_recv.at[0, c], wide_rsem.at[0, c])
        collect(0, c)

        def mix_loop(m, carry):
            for i in range(8):
                k = m * 8 + i
                real = rows[pl.ds(pl.multiple_of(k * 16, 16), 8), :]
                imag = rows[pl.ds(pl.multiple_of(k * 16 + 8, 8), 8), :]
                upper = jnp.concatenate([real, -imag], axis=1)
                lower = jnp.concatenate([imag, real], axis=1)
                paired = jnp.concatenate([upper, lower], axis=0).astype(bf16)
                pairs[c, k] = paired
                mixed[pl.ds(pl.multiple_of(k * 16, 16), 16), :] = dot(paired, weight[k, c]).astype(bf16)
            return carry

        lax.fori_loop(0, 2, mix_loop, 0)
        back_send[c] = dot(scatter[...], mixed[...]).astype(bf16).reshape(8, 32, 128)
        back_start(c)

    t4_load.wait()
    for c in range(2):
        for q in range(2):
            drain(back_recv.at[c, pl.ds(q * 8, 8)], back_rsem.at[c, q])
            values = back_recv[c, q * 8 : q * 8 + 8].reshape(256, 128)
            for e in range(2):
                ring_send[0, e, c, :, q] = dot_exact(t4[e], values).reshape(16, 16, 128).astype(bf16)
        plane_start(0, 0, c)
    plane_start(0, 1, 0)
    plane_sent(0, 0, 1)
    plane_start(0, 1, 1)

    t5_load.wait()
    t6_load.wait()
    up_load.wait()
    stores = []
    for e in range(2):
        for c in range(2):
            drain(ring_recv.at[0, e, c], ring_rsem.at[0, e, c])
            for q in range(2):
                first = c * 8 + q * 4
                values = ring_recv[0, e, c, :, q].reshape(256, 128)
                ybuf[first : first + 4] = dot_exact(t5[...], values).reshape(4, 128, 128)

        def cell_loop(m, carry):
            for i in range(16):
                k = m * 16 + i
                values = ybuf[:, pl.ds(pl.multiple_of(k * 8, 8), 8), :].reshape(128, 128)
                half = jnp.concatenate(split(values), axis=1)
                both = dot(t6[...], jnp.concatenate([half, half], axis=0))
                here = pl.ds(pl.multiple_of(k * 256, 256), 256)
                value, slope = gelu_pair(both[:, :128] + both[:, 128:] + base[e, here, :])
                out[e, here, :] = value.astype(bf16)
                depth_step(e, k, slope * up[e, here, :].astype(f32))
            return carry

        lax.fori_loop(0, 1, cell_loop, 0)
        store = pltpu.make_async_copy(out.at[e], out_hbm.at[e], store_sem.at[e])
        store.start()
        stores.append(store)
        for c in range(2):
            for q in range(2):
                ring_send[1, e, c, :, q] = row_step(e, c, q)
            if e == 1 and c == 0:
                plane_sent(1, 0, 0)
            if e == 1 and c == 1:
                plane_sent(1, 0, 1)
                plane_sent(1, 1, 0)
            plane_start(1, e, c)

    for c in range(2):
        for e in range(2):
            drain(ring_recv.at[1, e, c], ring_rsem.at[1, e, c])
        for q in range(2):
            plane_step(1, c, q, ring_recv[1, 0, c, :, q], ring_recv[1, 1, c, :, q])
            wide_start(1, c, q)

    for c in range(2):
        drain(wide_recv.at[1, c], wide_rsem.at[1, c])
        collect(1, c)
        scale = jnp.where(g == 0, 1.0, 2.0).astype(f32) if c == 0 else f32(2.0)

        for half in range(2):
            for k in range(half * 8, half * 8 + 8):
                cotangent = (rows[k * 16 : k * 16 + 16, :] * scale).astype(bf16)
                product = lax.dot_general(
                    pairs[c, k], cotangent, (((0,), (0,)), ((), ())), preferred_element_type=f32
                )
                grad[c, k] = product.astype(bf16)
            part = pl.ds(half * 8, 8)
            store = pltpu.make_async_copy(grad.at[c, part], grad_hbm.at[part, c], store_sem.at[2 + 2 * c + half])
            store.start()
            stores.append(store)

    for n in range(2):
        for c in range(2):
            for q in range(2):
                wide_drain(n, c, q)
    for e, c in ((0, 0), (1, 0), (1, 1)):
        plane_sent(0, e, c)
    for c in range(2):
        first_sent(1, c)
    plane_sent(1, 1, 1)
    for c in range(2):
        drain(back_recv.at[c, pl.ds(0, 15)], back_ssem.at[c])
    for store in stores:
        store.wait()


def shards(tables, field, upstream, mode_weights, skip_weight, channel_bias):
    anywhere = pl.BlockSpec(memory_space=pl.ANY)
    out, grad = pl.pallas_call(
        kernel,
        out_shape=(
            jax.ShapeDtypeStruct((2, 4096, 128), bf16),
            jax.ShapeDtypeStruct((16, 2, 256, 128), bf16),
        ),
        in_specs=[anywhere] * 13,
        out_specs=(anywhere, anywhere),
        scratch_shapes=[
            pltpu.VMEM((2, 4096, 128), f32),
            pltpu.VMEM((2, 4096, 128), bf16),
            pltpu.VMEM((16, 2, 256, 128), bf16),
            pltpu.VMEM((128, 128), f32),
            pltpu.VMEM((1, 128), f32),
            pltpu.VMEM((256, 256), bf16),
            pltpu.VMEM((256, 256), bf16),
            pltpu.VMEM((2, 512, 256), bf16),
            pltpu.VMEM((2, 512, 256), bf16),
            pltpu.VMEM((1024, 256), bf16),
            pltpu.VMEM((256, 256), bf16),
            pltpu.VMEM((256, 512), bf16),
            pltpu.VMEM((256, 256), bf16),
            pltpu.VMEM((2, 4096, 128), f32),
            pltpu.VMEM((2, 4096, 128), bf16),
            pltpu.VMEM((2, 16, 256, 128), bf16),
            pltpu.VMEM((2, 16, 128, 128), f32),
            pltpu.VMEM((16, 128, 128), f32),
            pltpu.VMEM((256, 128), f32),
            pltpu.VMEM((2, 16, 16, 256), bf16),
            pltpu.VMEM((256, 128), bf16),
            pltpu.VMEM((2, 2, 16, 2, 16, 128), bf16),
            pltpu.VMEM((2, 2, 16, 2, 16, 128), bf16),
            pltpu.VMEM((2, 2, 2, 16, 2, 16, 128), bf16),
            pltpu.VMEM((2, 2, 2, 16, 2, 16, 128), bf16),
            pltpu.VMEM((2, 2, 2, 8, 32, 128), f32),
            pltpu.VMEM((2, 2, 16, 32, 128), f32),
            pltpu.VMEM((2, 8, 32, 128), bf16),
            pltpu.VMEM((2, 16, 32, 128), bf16),
            pltpu.SemaphoreType.DMA((20,)),
            pltpu.SemaphoreType.DMA((2, 2)),
            pltpu.SemaphoreType.DMA((2, 2)),
            pltpu.SemaphoreType.DMA((2, 2, 2)),
            pltpu.SemaphoreType.DMA((2, 2, 2)),
            pltpu.SemaphoreType.DMA((2, 2, 2)),
            pltpu.SemaphoreType.DMA((2, 2)),
            pltpu.SemaphoreType.DMA((2,)),
            pltpu.SemaphoreType.DMA((2, 2)),
            pltpu.SemaphoreType.DMA((6,)),
        ],
        compiler_params=pltpu.CompilerParams(
            collective_id=0, has_side_effects=True, vmem_limit_bytes=63 * 1024 * 1024
        ),
    )(
        field.reshape(2, 4096, 128),
        upstream.reshape(2, 4096, 128),
        mode_weights.reshape(16, 2, 256, 128),
        skip_weight,
        channel_bias.reshape(1, 128),
        *[jnp.asarray(table) for table in tables],
    )
    return out.reshape(1, 2, 64, 64, 128), grad.reshape(16, 1, 2, 2, 128, 128)


def solution(mesh):
    in_specs = (
        P("grp", "pen", None, None, None),
        P("grp", "pen", None, None, None),
        P(None, "pen", "grp", None, None, None),
        P(),
        P(),
    )
    out_specs = (P("grp", "pen", None, None, None), P(None, "pen", "grp", None, None, None))
    return jax.shard_map(
        functools.partial(shards, make_tables()), mesh=mesh, in_specs=in_specs, out_specs=out_specs, check_vma=False
    )
```
